32 devices in a mesh: groups: 2 (over y), dp: 4 (over x, core), head: 4 (over z).
Axes of the slice: x: 2, y: 2, z: 4, core: 2. Of those that a mesh axis runs over, the one named last changes fastest.
Arguments:
- train_grads: bfloat16 [2, 32, 256, 8192], P(None, ('groups', 'dp'), None, 'head'), parts along dimension 1, may hold values from -6 to 6
- train_acts: bfloat16 [2, 32, 256, 8192], P(None, ('groups', 'dp'), None, 'head'), parts along dimension 1, may hold values from -6 to 6
- train_ids: int32 [32, 256], P(('groups', 'dp')), parts along dimension 0, may hold values from 0 to 128255
- query_grads: bfloat16 [2, 8, 256, 8192], P(None, ('groups', 'dp'), None, 'head'), parts along dimension 1, may hold values from -6 to 6
- query_acts: bfloat16 [2, 8, 256, 8192], P(None, ('groups', 'dp'), None, 'head'), parts along dimension 1, may hold values from -6 to 6
- query_ids: int32 [8, 256], P(('groups', 'dp')), parts along dimension 0, may hold values from 0 to 128255
- token_weight: float32 [128256], replicated, may hold values from 0.25 to 4
- out_proj: bfloat16 [2, 64, 8192], P(None, None, 'head'), may hold values from -0.0625 to 0.0625
- in_proj: bfloat16 [2, 64, 64, 128], P(None, 'head'), may hold values from -0.5 to 0.5
- out_factor: float32 [2, 64, 64], replicated, as said below
- in_factor: float32 [2, 64, 64, 64], P(None, 'head'), as said below
Outputs:
- scores: float32 [4, 32], P(None, ('groups', 'dp')), parts along dimension 1
The draws below stay inside these ranges and needn't reach their ends.
There are 2 independent parts, one for each index of `groups`. The reference program is written for one: setup_inputs(seed, part) draws one part's arguments, and reference() takes and returns one part's arrays. A program takes and returns all parts, laid end to end along the dimension named above; an argument that names none is the same for every part. Nothing has to cross between parts.
Inputs may be any that keep to these rules, and one draw needn't show every extreme that they name: out_factor and in_factor are symmetric matrices. in_factor matrices are symmetric.
All inputs are finite; a program needn't handle non-finite values.
Results may differ from the reference program's by a relative error of at most 0.0053.
Values sent between devices are 32-bit elements; how exact they have to be, the bound alone decides.
No kernel may reach another device: no remote copies, remote signals or barrier semaphores. Data moves between devices by JAX's collectives and lax.ppermute only.
A program may use at most 128 MiB of HBM per device.

```python
import math
import jax
import jax.numpy as jnp
import numpy as np
from jax import lax

D = 8192
HEADS = 64
HD = 128
VOCAB = 128256
RANK = 64
LAYERS = 2
LEN = 256
NTRAIN = 16
NQUERY = 4


def symmetric_factor(key, shape):
    diag_key, off_key = jax.random.split(key)
    noise = jax.random.normal(off_key, shape, jnp.float32) * (0.5 / math.sqrt(RANK))
    noise = (noise + jnp.swapaxes(noise, -1, -2)) * 0.7071
    diag_vals = jax.random.uniform(diag_key, shape[:-1], jnp.float32, 1.0, 2.0)
    eye = jnp.eye(RANK, dtype=jnp.float32)
    return noise * (1.0 - eye) + diag_vals[..., None] * eye


def draw_out_factor(key, part):
    key = jax.random.fold_in(key, 11)
    return symmetric_factor(key, (LAYERS, RANK, RANK))


def draw_in_factor(key, part):
    key = jax.random.fold_in(key, 23)
    return symmetric_factor(key, (LAYERS, HEADS, RANK, RANK))


def set_ends(array, own_key, least, high):
    longest = array.shape.index(max(array.shape))
    spots = []
    for shift in (0, 1):
        where = [jax.random.randint(jax.random.fold_in(own_key, axis), (), 0, length) for axis, length in enumerate(array.shape)]
        where[longest] = (where[longest] + shift) % array.shape[longest]
        spots.append(tuple(where))
    return array.at[spots[0]].set(least).at[spots[1]].set(high)


def block_levels(key, extent, cuts, low, high):
    gain = 1.0
    for dim, blocks in cuts:
        heights = jax.random.uniform(jax.random.fold_in(jax.random.fold_in(key, 6), dim), (blocks,), jnp.float32, low / len(cuts), high / len(cuts))
        gain = gain * jnp.repeat(jnp.exp(heights), extent[dim] // blocks).reshape((-1,) + (1,) * (len(extent) - 1 - dim))
    return gain


def ranked_wide(stream_key, shape, amount, skew):
    portions = [min(1 << octave, amount + 1 - (1 << octave)) * (1 << 20) // math.isqrt((1 << octave) ** skew) + 1 for octave in range((amount + 1).bit_length()) if 1 << octave <= amount]
    scale = 1 + sum(portions) // (1 << 30)
    listing = np.cumsum(np.array([max(1, weight // scale) for weight in portions]))
    lot = jax.random.randint(jax.random.fold_in(stream_key, 1), shape, 0, int(listing[len(portions) - 1]))
    start = jnp.left_shift(1, jnp.searchsorted(jnp.asarray(listing, jnp.int32), lot, side="right").astype(jnp.int32))
    grade = start - 1 + jax.random.randint(jax.random.fold_in(stream_key, 4), shape, 0, 1 << 30) % jnp.minimum(start, amount + 1 - start)
    return jax.random.permutation(jax.random.fold_in(stream_key, 2), amount)[grade].astype(jnp.int32)


def bell_draw(key, dims, spread, most, cuts=(), held_as=jnp.bfloat16):
    level = block_levels(key, dims, cuts, -0.22, 0.18) if cuts else 1.0
    values = jax.random.normal(key, dims, jnp.float32) * spread * level
    return jnp.minimum(jnp.maximum(values, -most), most).astype(held_as)


def setup_inputs(seed: int = 0, part: int = 0) -> dict:
    splits = jax.random.split(jax.random.key(seed), 12)
    part_splits = jax.random.split(jax.random.fold_in(splits[11], part), 12)
    train_grads = bell_draw(part_splits[0], (LAYERS, NTRAIN, LEN, D), 1.0, 6.0, ((1, 4), (3, 4)))
    train_acts = bell_draw(part_splits[1], (LAYERS, NTRAIN, LEN, HEADS * HD), 1.0, 6.0, ((1, 4), (3, 4)))
    train_ids = set_ends(ranked_wide(part_splits[2], (NTRAIN, LEN), VOCAB, 2), jax.random.fold_in(part_splits[2], 3), 0, VOCAB - 1).astype(jnp.int32)
    query_grads = bell_draw(part_splits[3], (LAYERS, NQUERY, LEN, D), 1.0, 6.0, ((1, 4), (3, 4)))
    query_acts = bell_draw(part_splits[4], (LAYERS, NQUERY, LEN, HEADS * HD), 1.0, 6.0, ((1, 4), (3, 4)))
    query_ids = set_ends(ranked_wide(part_splits[5], (NQUERY, LEN), VOCAB, 2), jax.random.fold_in(part_splits[5], 3), 0, VOCAB - 1).astype(jnp.int32)
    token_weight = jnp.clip(jnp.exp(jax.random.uniform(splits[6], (VOCAB,), jnp.float32, math.log(0.25), math.log(4.0))), 0.25, 4.0)
    out_proj = bell_draw(splits[7], (LAYERS, RANK, D), D ** -0.5, 0.0625, ((2, 4),))
    in_proj = bell_draw(splits[8], (LAYERS, HEADS, RANK, HD), HD ** -0.5, 0.5, ((1, 4),))
    out_factor = draw_out_factor(jax.random.fold_in(splits[11], 71), part)
    in_factor = draw_in_factor(jax.random.fold_in(splits[11], 71), part)
    return dict(train_grads=train_grads, train_acts=train_acts, train_ids=train_ids, query_grads=query_grads, query_acts=query_acts, query_ids=query_ids, token_weight=token_weight, out_proj=out_proj, in_proj=in_proj, out_factor=out_factor, in_factor=in_factor)


HIGH = lax.Precision.HIGHEST

def gradient_blocks(grads_in, acts_in, ids, token_weight, out_proj, in_proj):
    count = ids.shape[0]
    scale = token_weight[ids].reshape(-1, 1)
    result = []
    for layer_idx in range(LAYERS):
        out_side = jnp.dot(grads_in[layer_idx].reshape(count * LEN, D), out_proj[layer_idx].T, preferred_element_type=jnp.float32)
        acts_flat = acts_in[layer_idx].reshape(count * LEN, HEADS, HD).astype(jnp.float32)
        in_side = jnp.einsum('thk,hrk->thr', acts_flat, in_proj[layer_idx].astype(jnp.float32), precision=HIGH)
        in_side = in_side.astype(jnp.bfloat16).astype(jnp.float32)
        weighted = (out_side * scale).astype(jnp.bfloat16).astype(jnp.float32).reshape(count, LEN, RANK)
        blocks = jnp.einsum('ntr,nths->nhrs', weighted, in_side.reshape(count, LEN, HEADS, RANK), precision=HIGH)
        result.append(blocks / math.sqrt(LEN))
    return jnp.stack(result)

def reference(train_grads, train_acts, train_ids, query_grads, query_acts, query_ids, token_weight, out_proj, in_proj, out_factor, in_factor):
    train_blocks = gradient_blocks(train_grads, train_acts, train_ids, token_weight, out_proj, in_proj)
    query_blocks = gradient_blocks(query_grads, query_acts, query_ids, token_weight, out_proj, in_proj)
    left = jnp.einsum('lij,lnhjk->lnhik', out_factor, train_blocks, precision=HIGH)
    prepared = jnp.einsum('lnhik,lhkm->lnhim', left, in_factor, precision=HIGH)
    total = jnp.einsum('lqhij,lnhij->qn', query_blocks, prepared, precision=HIGH)
    return total / math.sqrt(LAYERS * HEADS * RANK * RANK)
```

```python
import math

import jax
import jax.numpy as jnp
from jax import lax
from jax.experimental import pallas as pl
from jax.experimental.pallas import tpu as pltpu
from jax.sharding import PartitionSpec as P

HIGH = lax.Precision.HIGHEST
F32 = jnp.float32
BF16 = jnp.bfloat16
NT = (((1,), (1,)), ((), ()))
VMEM_LIMIT = 48 * 1024 * 1024

NEAR = [(0, 1), (1, 0), (2, 3), (3, 2)]
FAR = [(0, 2), (2, 0), (1, 3), (3, 1)]


def params():
    return pltpu.CompilerParams(vmem_limit_bytes=VMEM_LIMIT)


def cost(flops, nbytes):
    return pl.CostEstimate(flops=int(flops), bytes_accessed=int(nbytes), transcendentals=0)


def side_kernel(layer_ref, grads_ref, proj_ref, out_ref):
    side = lax.dot_general(grads_ref[0, 0], proj_ref[0], NT, preferred_element_type=F32)
    out_ref[0] = side.T


def side_partial(layer, grads, out_proj):
    _, count, length, feats = grads.shape
    rank = out_proj.shape[1]
    return pl.pallas_call(
        side_kernel,
        out_shape=jax.ShapeDtypeStruct((count, rank, length), F32),
        grid_spec=pltpu.PrefetchScalarGridSpec(
            num_scalar_prefetch=1,
            grid=(count,),
            in_specs=[
                pl.BlockSpec((1, 1, length, feats), lambda i, l: (l[0], i, 0, 0)),
                pl.BlockSpec((1, rank, feats), lambda i, l: (l[0], 0, 0)),
            ],
            out_specs=pl.BlockSpec((1, rank, length), lambda i, l: (i, 0, 0)),
        ),
        compiler_params=params(),
        cost_estimate=cost(
            2 * count * length * feats * 256, 2 * (count * length + rank) * feats
        ),
        name="side_partial",
    )(layer, grads, out_proj)


def in_kernel(acts_ref, proj_ref, out_ref):
    heads, rank, width = proj_ref.shape[1:]
    none = jnp.zeros((rank, width), BF16)
    for pair in range(heads // 2):
        one, two = proj_ref[0, 2 * pair], proj_ref[0, 2 * pair + 1]
        both = jnp.concatenate(
            [jnp.concatenate([one, none], axis=1), jnp.concatenate([none, two], axis=1)], axis=0
        )
        acts = acts_ref[0, 0, :, 2 * width * pair : 2 * width * (pair + 1)]
        side = lax.dot_general(acts, both, NT, preferred_element_type=F32)
        out_ref[0, 0, :, 2 * rank * pair : 2 * rank * (pair + 1)] = side.astype(BF16)


def in_side(acts, in_proj):
    layers, count, length, feats = acts.shape
    _, heads, rank, width = in_proj.shape
    return pl.pallas_call(
        in_kernel,
        out_shape=jax.ShapeDtypeStruct((layers, count, length, heads * rank), BF16),
        grid=(layers, count),
        in_specs=[
            pl.BlockSpec((1, 1, length, feats), lambda l, i: (l, i, 0, 0)),
            pl.BlockSpec((1, heads, rank, width), lambda l, i: (l, 0, 0, 0)),
        ],
        out_specs=pl.BlockSpec((1, 1, length, heads * rank), lambda l, i: (l, i, 0, 0)),
        compiler_params=params(),
        cost_estimate=cost(
            2 * layers * count * length * feats * 128, 3 * layers * count * length * feats
        ),
        name="in_side",
    )(acts, in_proj)


def token_kernel(ids_ref, table_ref, out_ref):
    table = table_ref[...]
    rows, lanes = table.shape
    high = table.astype(BF16)
    rest = table - high.astype(F32)
    mid = rest.astype(BF16)
    low = (rest - mid.astype(F32)).astype(BF16)
    turned = [part.T for part in (high, mid, low)]
    length = ids_ref.shape[1]
    for row in range(ids_ref.shape[0]):
        ids = ids_ref[row : row + 1, :]
        block = ids // lanes
        at = lax.broadcasted_iota(jnp.int32, (rows, length), 0) == block
        hot = jnp.where(at, 1.0, 0.0).astype(BF16)
        picked = sum(jnp.dot(part, hot, preferred_element_type=F32) for part in turned)
        lane = lax.broadcasted_iota(jnp.int32, (lanes, length), 0) == ids - block * lanes
        out_ref[row : row + 1, :] = jnp.sum(
            jnp.where(lane, picked, 0.0), axis=0, keepdims=True
        )


def token_scale(ids, token_weight):
    lanes = 128
    table = jnp.pad(token_weight, (0, -token_weight.shape[0] % lanes)).reshape(-1, lanes)
    return pl.pallas_call(
        token_kernel,
        out_shape=jax.ShapeDtypeStruct(ids.shape, F32),
        compiler_params=params(),
        cost_estimate=cost(6 * ids.size * table.size, 4 * table.size),
        name="token_scale",
    )(ids, table)


def weighted_blocks(side, scale, in_side_seq, length):
    weighted = (side * scale).astype(BF16)
    return jnp.dot(weighted, in_side_seq, preferred_element_type=F32) * (1.0 / math.sqrt(length))


def blocks_kernel(layer_ref, side_ref, scale_ref, in_ref, out_ref):
    out_ref[0] = weighted_blocks(side_ref[0], scale_ref[0], in_ref[0, 0], side_ref.shape[2])


def train_blocks(layer, side, scale, in_sides):
    count, rank, length = side.shape
    wide = in_sides.shape[3]
    return pl.pallas_call(
        blocks_kernel,
        out_shape=jax.ShapeDtypeStruct((count, rank, wide), F32),
        grid_spec=pltpu.PrefetchScalarGridSpec(
            num_scalar_prefetch=1,
            grid=(count,),
            in_specs=[
                pl.BlockSpec((1, rank, length), lambda i, l: (i, 0, 0)),
                pl.BlockSpec((1, 1, length), lambda i, l: (i, 0, 0)),
                pl.BlockSpec((1, 1, length, wide), lambda i, l: (l[0], i, 0, 0)),
            ],
            out_specs=pl.BlockSpec((1, rank, wide), lambda i, l: (i, 0, 0)),
        ),
        compiler_params=params(),
        cost_estimate=cost(
            8 * count * rank * length * wide, count * (2 * length + 4 * rank) * wide
        ),
        name="train_blocks",
    )(layer, side, scale.reshape(count, 1, length), in_sides)


def query_kernel(layer_ref, side_ref, scale_ref, in_ref, out_factor_ref, in_factor_ref, out_ref):
    heads, rank = in_factor_ref.shape[1], in_factor_ref.shape[2]
    blocks = weighted_blocks(side_ref[0], scale_ref[0], in_ref[0, 0], side_ref.shape[2])
    left = jnp.dot(out_factor_ref[0], blocks, precision=HIGH, preferred_element_type=F32)
    none = jnp.zeros((rank, rank), F32)
    for pair in range(heads // 2):
        one, two = in_factor_ref[0, 2 * pair], in_factor_ref[0, 2 * pair + 1]
        both = jnp.concatenate(
            [jnp.concatenate([one, none], axis=1), jnp.concatenate([none, two], axis=1)], axis=0
        )
        span = slice(2 * rank * pair, 2 * rank * (pair + 1))
        out_ref[0, :, span] = jnp.dot(
            left[:, span], both, precision=HIGH, preferred_element_type=F32
        )


def query_ready(layer, side, scale, in_sides, out_factor, in_factor):
    count, rank, length = side.shape
    wide = in_sides.shape[3]
    heads = in_factor.shape[1]
    return pl.pallas_call(
        query_kernel,
        out_shape=jax.ShapeDtypeStruct((count, rank, wide), F32),
        grid_spec=pltpu.PrefetchScalarGridSpec(
            num_scalar_prefetch=1,
            grid=(count,),
            in_specs=[
                pl.BlockSpec((1, rank, length), lambda i, l: (i, 0, 0)),
                pl.BlockSpec((1, 1, length), lambda i, l: (i, 0, 0)),
                pl.BlockSpec((1, 1, length, wide), lambda i, l: (l[0], i, 0, 0)),
                pl.BlockSpec((1, rank, rank), lambda i, l: (l[0], 0, 0)),
                pl.BlockSpec((1, heads, rank, rank), lambda i, l: (l[0], 0, 0, 0)),
            ],
            out_specs=pl.BlockSpec((1, rank, wide), lambda i, l: (i, 0, 0)),
        ),
        compiler_params=params(),
        cost_estimate=cost(
            20 * count * rank * length * wide, count * (2 * length + 4 * rank) * wide
        ),
        name="query_ready",
    )(layer, side, scale.reshape(count, 1, length), in_sides, out_factor, in_factor)


def score_kernel(groups, *refs):
    out_ref = refs[-1]
    at = 0
    lanes = out_ref.shape[1]
    total = None
    for queries_n in groups:
        query_refs = refs[at : at + queries_n]
        blocks_ref = refs[at + queries_n]
        at += queries_n + 1
        rows = []
        for query_ref in query_refs:
            for query_idx in range(query_ref.shape[0]):
                query = query_ref[query_idx]
                row = jnp.zeros((1, lanes), F32)
                for seq in range(blocks_ref.shape[0]):
                    product = jnp.sum(query * blocks_ref[seq], axis=0, keepdims=True)
                    value = jnp.sum(product, axis=1, keepdims=True)
                    lane = lax.broadcasted_iota(jnp.int32, (1, lanes), 1)
                    row = jnp.where(lane == seq, value, row)
                rows.append(row)
        stacked = jnp.concatenate(rows, axis=0)
        total = stacked if total is None else total + stacked
    out_ref[...] = total


def score_terms(pairs):
    rows = sum(query.shape[0] for query in pairs[0][0])
    flat = [array for queries, blocks in pairs for array in (*queries, blocks)]
    groups = tuple(len(queries) for queries, _ in pairs)
    return pl.pallas_call(
        lambda *refs: score_kernel(groups, *refs),
        out_shape=jax.ShapeDtypeStruct((rows, 128), F32),
        compiler_params=params(),
        cost_estimate=cost(
            sum(2 * rows * blocks.size for _, blocks in pairs), sum(4 * a.size for a in flat)
        ),
        name="score_terms",
    )(*flat)


def local(
    train_grads,
    train_acts,
    train_ids,
    query_grads,
    query_acts,
    query_ids,
    token_weight,
    out_proj,
    in_proj,
    out_factor,
    in_factor,
):
    layers, train_n = train_grads.shape[:2]
    heads, rank = in_proj.shape[1:3]
    n_head, n_dp = lax.axis_size("head"), lax.axis_size("dp")
    by_pairs = n_head == 4 and n_dp == 4 and layers == 2 and query_ids.shape[0] == 1
    norm = 1.0 / math.sqrt(layers * heads * n_head * rank * rank)

    def layer_at(idx):
        return jnp.full((1,), idx, jnp.int32)

    def near(array, axis="head"):
        return lax.ppermute(array, axis, NEAR)

    def far(array, axis="head"):
        return lax.ppermute(array, axis, FAR)

    if by_pairs:
        mine = (lax.axis_index("head") % 2).astype(jnp.int32).reshape(1)
        order = [mine, 1 - mine]

        def summed(grads):
            sent = near(side_partial(order[1], grads, out_proj))
            pair = side_partial(order[0], grads, out_proj) + sent
            whole = pair + far(pair)
            return [whole, near(whole)]
    else:
        order = [layer_at(idx) for idx in range(layers)]

        def summed(grads):
            return [lax.psum(side_partial(at, grads, out_proj), "head") for at in order]

    query_sides = summed(query_grads)
    train_sides = summed(train_grads)
    query_in = in_side(query_acts, in_proj)
    scale = token_scale(jnp.concatenate([query_ids, train_ids]), token_weight)
    query_scale, train_scale = scale[: query_ids.shape[0]], scale[query_ids.shape[0] :]
    train_in = in_side(train_acts, in_proj)

    pairs = []
    for at, query_side, train_side in zip(order, query_sides, train_sides):
        ready = query_ready(at, query_side, query_scale, query_in, out_factor, in_factor)
        if by_pairs:
            across = far(ready, "dp")
            every = [ready, near(ready, "dp"), across, near(across, "dp")]
        else:
            every = [lax.all_gather(ready, "dp", axis=0, tiled=True)]
        pairs.append((every, train_blocks(at, train_side, train_scale, train_in)))
    terms = score_terms(pairs)

    if by_pairs:
        terms = terms[jnp.arange(4) ^ lax.axis_index("dp")]
        total = terms
        for shift in range(1, 4):
            total = total + lax.ppermute(
                terms, "head", [(idx, (idx + shift) % 4) for idx in range(4)]
            )
    else:
        total = lax.psum(terms, "head")
    return total[:, :train_n] * norm


def solution(mesh):
    return jax.shard_map(
        local,
        mesh=mesh,
        in_specs=(
            P(None, ("groups", "dp"), None, "head"),
            P(None, ("groups", "dp"), None, "head"),
            P(("groups", "dp"), None),
            P(None, ("groups", "dp"), None, "head"),
            P(None, ("groups", "dp"), None, "head"),
            P(("groups", "dp"), None),
            P(),
            P(None, None, "head"),
            P(None, "head", None, None),
            P(),
            P(None, "head", None, None),
        ),
        out_specs=P(None, ("groups", "dp")),
        check_vma=False,
    )
```

```python
import functools
import math

import jax
import jax.numpy as jnp
from jax import lax
from jax.experimental import pallas as pl
from jax.experimental.pallas import tpu as pltpu
from jax.sharding import PartitionSpec as P

HIGH = lax.Precision.HIGHEST
F32 = jnp.float32
BF16 = jnp.bfloat16
NT = (((1,), (1,)), ((), ()))
VMEM_LIMIT = 24 * 1024 * 1024
SCALE = 1.0

NEAR = [(0, 1), (1, 0), (2, 3), (3, 2)]
FAR = [(0, 2), (2, 0), (1, 3), (3, 1)]

WHOLE = pl.BlockSpec(memory_space=pltpu.VMEM)
IN_HBM = pl.BlockSpec(memory_space=pltpu.HBM)


def call(kernel, inputs, out_shape, name, *, micros, after=(), prefetch=(), grid=(1,),
         in_specs=None, out_specs=None, scratch=(), mebibytes=8):
    skip = len(prefetch) + len(inputs)

    def body(*refs):
        return kernel(*refs[:skip], *refs[skip + len(after) :])

    in_specs = in_specs or [WHOLE] * len(inputs)
    return pl.pallas_call(
        body,
        out_shape=out_shape,
        grid_spec=pltpu.PrefetchScalarGridSpec(
            num_scalar_prefetch=len(prefetch),
            grid=grid,
            in_specs=[*in_specs, *[pl.BlockSpec(memory_space=pl.ANY)] * len(after)],
            out_specs=out_specs or WHOLE,
            scratch_shapes=scratch,
        ),
        compiler_params=pltpu.CompilerParams(vmem_limit_bytes=mebibytes << 20),
        cost_estimate=pl.CostEstimate(
            flops=int(micros * SCALE * 1.1e9), bytes_accessed=0, transcendentals=0
        ),
        name=name,
    )(*prefetch, *inputs, *after)


def side_kernel(layer_ref, grads_ref, proj_ref, out_ref):
    side = lax.dot_general(grads_ref[0, 0], proj_ref[0], NT, preferred_element_type=F32)
    out_ref[0] = side.T


def side_partial(layer, grads, out_proj, micros, after=()):
    _, count, length, feats = grads.shape
    rank = out_proj.shape[1]
    return call(
        side_kernel,
        [grads, out_proj],
        jax.ShapeDtypeStruct((count, rank, length), F32),
        "side_partial",
        micros=micros,
        after=after,
        prefetch=[layer],
        grid=(count,),
        in_specs=[
            pl.BlockSpec((1, 1, length, feats), lambda i, l: (l[0], i, 0, 0)),
            pl.BlockSpec((1, rank, feats), lambda i, l: (l[0], 0, 0)),
        ],
        out_specs=pl.BlockSpec((1, rank, length), lambda i, l: (i, 0, 0)),
    )


def first_kernel(layer_ref, grads_hbm, proj_hbm, out_ref, grads, proj, sems):
    layer = layer_ref[0]
    copies = [
        pltpu.make_async_copy(grads_hbm.at[layer], grads, sems.at[0]),
        pltpu.make_async_copy(proj_hbm.at[layer], proj, sems.at[1]),
    ]
    for copy in copies:
        copy.start()
    for copy in copies:
        copy.wait()
    for seq in range(grads.shape[0]):
        out_ref[seq] = lax.dot_general(grads[seq], proj[...], NT, preferred_element_type=F32).T


def first_partial(layer, grads, out_proj, micros):
    _, count, length, feats = grads.shape
    rank = out_proj.shape[1]
    return call(
        first_kernel,
        [pltpu.with_memory_space_constraint(array, pltpu.HBM) for array in (grads, out_proj)],
        jax.ShapeDtypeStruct((count, rank, length), F32),
        "first_partial",
        micros=micros,
        prefetch=[layer],
        in_specs=[IN_HBM, IN_HBM],
        scratch=[
            pltpu.VMEM((count, length, feats), BF16),
            pltpu.VMEM((rank, feats), BF16),
            pltpu.SemaphoreType.DMA((2,)),
        ],
    )


def in_kernel(acts_ref, proj_ref, out_ref):
    heads, rank, width = proj_ref.shape[1:]
    none = jnp.zeros((rank, width), BF16)
    for pair in range(heads // 2):
        one, two = proj_ref[0, 2 * pair], proj_ref[0, 2 * pair + 1]
        both = jnp.concatenate(
            [jnp.concatenate([one, none], axis=1), jnp.concatenate([none, two], axis=1)], axis=0
        )
        acts = acts_ref[0, 0, :, 2 * width * pair : 2 * width * (pair + 1)]
        side = lax.dot_general(acts, both, NT, preferred_element_type=F32)
        out_ref[0, 0, :, 2 * rank * pair : 2 * rank * (pair + 1)] = side.astype(BF16)


def in_side(acts, in_proj, micros, after=()):
    layers, count, length, feats = acts.shape
    _, heads, rank, width = in_proj.shape
    return call(
        in_kernel,
        [acts, in_proj],
        jax.ShapeDtypeStruct((layers, count, length, heads * rank), BF16),
        "in_side",
        micros=micros,
        after=after,
        grid=(layers, count),
        in_specs=[
            pl.BlockSpec((1, 1, length, feats), lambda l, i: (l, i, 0, 0)),
            pl.BlockSpec((1, heads, rank, width), lambda l, i: (l, 0, 0, 0)),
        ],
        out_specs=pl.BlockSpec((1, 1, length, heads * rank), lambda l, i: (l, i, 0, 0)),
    )


def streamed_kernel(layer_ref, acts_hbm, proj_ref, one_ref, two_ref, tick_ref, acts, sems):
    layers, count = acts.shape[:2]
    order = [layer_ref[0], 1 - layer_ref[0]]
    heads, rank, width = proj_ref.shape[1:]
    steps = [(layer, seq) for layer in range(layers) for seq in range(count)]

    def copy(step):
        layer, seq = steps[step]
        return pltpu.make_async_copy(
            acts_hbm.at[order[layer], seq], acts.at[layer, seq], sems.at[step]
        )

    for step in range(len(steps)):
        copy(step).start()
    none = jnp.zeros((rank, width), BF16)
    for step, (layer, seq) in enumerate(steps):
        copy(step).wait()
        for pair in range(heads // 2):
            one, two = proj_ref[order[layer], 2 * pair], proj_ref[order[layer], 2 * pair + 1]
            both = jnp.concatenate(
                [jnp.concatenate([one, none], axis=1), jnp.concatenate([none, two], axis=1)],
                axis=0,
            )
            pair_acts = acts[layer, seq, :, 2 * width * pair : 2 * width * (pair + 1)]
            side = lax.dot_general(pair_acts, both, NT, preferred_element_type=F32)
            span = slice(2 * rank * pair, 2 * rank * (pair + 1))
            (one_ref, two_ref)[layer][0, seq, :, span] = side.astype(BF16)
    tick_ref[...] = jnp.zeros_like(tick_ref)


def in_side_streamed(layer, acts, in_proj, micros, after=()):
    layers, count, length, feats = acts.shape
    _, heads, rank, width = in_proj.shape
    return call(
        streamed_kernel,
        [pltpu.with_memory_space_constraint(acts, pltpu.HBM), in_proj],
        [
            jax.ShapeDtypeStruct((1, count, length, heads * rank), BF16),
            jax.ShapeDtypeStruct((1, count, length, heads * rank), BF16),
            jax.ShapeDtypeStruct((8, 128), F32),
        ],
        "in_side_streamed",
        micros=micros,
        mebibytes=20,
        prefetch=[layer],
        after=after,
        in_specs=[IN_HBM, WHOLE],
        out_specs=[WHOLE] * 3,
        scratch=[
            pltpu.VMEM(acts.shape, BF16),
            pltpu.SemaphoreType.DMA((layers * count,)),
        ],
    )


def settle_kernel(one_ref, two_ref, out_ref):
    out_ref[...] = one_ref[...] + two_ref[...]


def settle(one, two, after):
    return call(
        settle_kernel, [one, two], jax.ShapeDtypeStruct(one.shape, F32), "settle", micros=0.2,
        after=after,
    )


def token_kernel(ids_ref, table_ref, out_ref):
    table = table_ref[...]
    rows, lanes = table.shape
    high = table.astype(BF16)
    rest = table - high.astype(F32)
    mid = rest.astype(BF16)
    low = (rest - mid.astype(F32)).astype(BF16)
    turned = [part.T for part in (high, mid, low)]
    length = ids_ref.shape[1]
    for row in range(ids_ref.shape[0]):
        ids = ids_ref[row : row + 1, :]
        block = ids // lanes
        at = lax.broadcasted_iota(jnp.int32, (rows, length), 0) == block
        hot = jnp.where(at, 1.0, 0.0).astype(BF16)
        picked = sum(jnp.dot(part, hot, preferred_element_type=F32) for part in turned)
        lane = lax.broadcasted_iota(jnp.int32, (lanes, length), 0) == ids - block * lanes
        out_ref[row : row + 1, :] = jnp.sum(
            jnp.where(lane, picked, 0.0), axis=0, keepdims=True
        )


def token_scale(ids, token_weight, after=()):
    lanes = 128
    table = jnp.pad(token_weight, (0, -token_weight.shape[0] % lanes)).reshape(-1, lanes)
    return call(
        token_kernel,
        [ids, table],
        jax.ShapeDtypeStruct(ids.shape, F32),
        "token_scale",
        micros=1.5,
        after=after,
    )


def weighted_blocks(side, scale, in_side_seq, length):
    weighted = (side * scale).astype(BF16)
    return jnp.dot(weighted, in_side_seq, preferred_element_type=F32) * (1.0 / math.sqrt(length))


def blocks_kernel(side_ref, scale_ref, in_ref, out_ref):
    out_ref[0] = weighted_blocks(side_ref[0], scale_ref[0], in_ref[0, 0], side_ref.shape[2])


def train_blocks(side, scale, in_sides, after=()):
    count, rank, length = side.shape
    wide = in_sides.shape[3]
    return call(
        blocks_kernel,
        [side, scale.reshape(count, 1, length), in_sides],
        jax.ShapeDtypeStruct((count, rank, wide), F32),
        "train_blocks",
        micros=0.9,
        after=after,
        grid=(count,),
        in_specs=[
            pl.BlockSpec((1, rank, length), lambda i: (i, 0, 0)),
            pl.BlockSpec((1, 1, length), lambda i: (i, 0, 0)),
            pl.BlockSpec((1, 1, length, wide), lambda i: (0, i, 0, 0)),
        ],
        out_specs=pl.BlockSpec((1, rank, wide), lambda i: (i, 0, 0)),
    )


def query_kernel(terms_n, layer_ref, *refs):
    terms, refs = refs[:terms_n], refs[terms_n:]
    scale_ref, in_ref, out_factor_ref, in_factor_ref, out_ref, side_ref = refs
    heads, rank = in_factor_ref.shape[1], in_factor_ref.shape[2]
    side = sum(term[0] for term in terms)
    side_ref[0] = side
    blocks = weighted_blocks(side, scale_ref[0], in_ref[0, 0], side.shape[1])
    left = jnp.dot(out_factor_ref[0], blocks, precision=HIGH, preferred_element_type=F32)
    none = jnp.zeros((rank, rank), F32)
    for pair in range(heads // 2):
        one, two = in_factor_ref[0, 2 * pair], in_factor_ref[0, 2 * pair + 1]
        both = jnp.concatenate(
            [jnp.concatenate([one, none], axis=1), jnp.concatenate([none, two], axis=1)], axis=0
        )
        span = slice(2 * rank * pair, 2 * rank * (pair + 1))
        out_ref[0, :, span] = jnp.dot(
            left[:, span], both, precision=HIGH, preferred_element_type=F32
        )


def query_ready(layer, terms, scale, in_sides, out_factor, in_factor, after=()):
    count, rank, length = terms[0].shape
    wide = in_sides.shape[3]
    heads = in_factor.shape[1]
    side_spec = pl.BlockSpec((1, rank, length), lambda i, l: (i, 0, 0))
    return call(
        functools.partial(query_kernel, len(terms)),
        [*terms, scale.reshape(count, 1, length), in_sides, out_factor, in_factor],
        [
            jax.ShapeDtypeStruct((count, rank, wide), F32),
            jax.ShapeDtypeStruct((count, rank, length), F32),
        ],
        "query_ready",
        micros=0.9,
        after=after,
        prefetch=[layer],
        grid=(count,),
        in_specs=[
            *[side_spec] * len(terms),
            pl.BlockSpec((1, 1, length), lambda i, l: (i, 0, 0)),
            pl.BlockSpec((1, 1, length, wide), lambda i, l: (l[0], i, 0, 0)),
            pl.BlockSpec((1, rank, rank), lambda i, l: (l[0], 0, 0)),
            pl.BlockSpec((1, heads, rank, rank), lambda i, l: (l[0], 0, 0, 0)),
        ],
        out_specs=[pl.BlockSpec((1, rank, wide), lambda i, l: (i, 0, 0)), side_spec],
    )


def score_kernel(groups, norm, flip_ref, *refs):
    out_ref = refs[-1]
    rows, lanes = out_ref.shape
    row_at = lax.broadcasted_iota(jnp.int32, (rows, lanes), 0)
    lane_at = lax.broadcasted_iota(jnp.int32, (rows, lanes), 1)
    total = jnp.zeros((rows, lanes), F32)
    at = 0
    for queries_n in groups:
        query_refs = refs[at : at + queries_n]
        blocks_ref = refs[at + queries_n]
        at += queries_n + 1
        queries = [(ref, idx) for ref in query_refs for idx in range(ref.shape[0])]
        for row, (query_ref, idx) in enumerate(queries):
            mine = row_at == (row ^ flip_ref[0])
            query = query_ref[idx]
            for seq in range(blocks_ref.shape[0]):
                product = jnp.sum(query * blocks_ref[seq], axis=0, keepdims=True)
                value = jnp.sum(product, axis=1, keepdims=True) * norm
                total = total + jnp.where(mine & (lane_at == seq), value, 0.0)
    out_ref[...] = total


def score_terms(flip, norm, pairs):
    rows = sum(query.shape[0] for query in pairs[0][0])
    flat = [array for queries, blocks in pairs for array in (*queries, blocks)]
    groups = tuple(len(queries) for queries, _ in pairs)
    return call(
        lambda *refs: score_kernel(groups, norm, *refs),
        flat,
        jax.ShapeDtypeStruct((rows, 128), F32),
        "score_terms",
        micros=1.0,
        prefetch=[flip],
    )


def local(
    train_grads,
    train_acts,
    train_ids,
    query_grads,
    query_acts,
    query_ids,
    token_weight,
    out_proj,
    in_proj,
    out_factor,
    in_factor,
):
    layers, train_n = train_grads.shape[:2]
    query_n = query_ids.shape[0]
    heads, rank = in_proj.shape[1:3]
    n_head, n_dp = lax.axis_size("head"), lax.axis_size("dp")
    by_pairs = n_head == 4 and n_dp == 4 and layers == 2 and query_n == 1
    norm = 1.0 / math.sqrt(layers * heads * n_head * rank * rank)

    def scalar(idx):
        return jnp.asarray(idx, jnp.int32).reshape(1)

    def near(array, axis="head"):
        return lax.ppermute(array, axis, NEAR)

    def far(array, axis="head"):
        return lax.ppermute(array, axis, FAR)

    def ready(at, terms, after=()):
        return query_ready(at, terms, query_scale, query_in, out_factor, in_factor, after)

    if by_pairs:
        mine = scalar(lax.axis_index("head") % 2)
        other = 1 - mine
        query_out = first_partial(other, query_grads, out_proj, 5.0)
        query_got = near(query_out)
        query_keep = side_partial(mine, query_grads, out_proj, 0.5, [query_out])
        train_out = side_partial(other, train_grads, out_proj, 1.9, [query_keep])
        train_got = near(train_out)
        query_pair = query_keep + query_got
        query_far = far(query_pair)
        query_in = in_side(query_acts, in_proj, 0.9, [query_pair])
        query_scale = token_scale(query_ids, token_weight, [query_in])
        train_keep = side_partial(mine, train_grads, out_proj, 1.9, [query_scale])
        train_pair = train_keep + train_got
        ready_own, query_own = ready(mine, [query_pair, query_far], [train_pair])
        across_own = far(ready_own, "dp")
        ready_other, _ = ready(other, [near(query_own)], [ready_own])
        across_other = far(ready_other, "dp")
        train_scale = token_scale(train_ids, token_weight, [ready_other])
        train_own = train_pair + far(train_pair)
        train_other = near(train_own)
        *train_in, _ = in_side_streamed(mine, train_acts, in_proj, 5.0, [train_own])
        pairs = []
        for side, sides_in, query, across in (
            (train_own, train_in[0], ready_own, across_own),
            (train_other, train_in[1], ready_other, across_other),
        ):
            every = [query, near(query, "dp"), across, near(across, "dp")]
            pairs.append((every, train_blocks(side, train_scale, sides_in)))
        terms = score_terms(scalar(lax.axis_index("dp")), norm, pairs)
        total = terms
        for shift in range(1, 4):
            total = total + lax.ppermute(
                terms, "head", [(idx, (idx + shift) % 4) for idx in range(4)]
            )
    else:
        query_scale = token_scale(query_ids, token_weight)
        train_scale = token_scale(train_ids, token_weight)
        query_in = in_side(query_acts, in_proj, 0.9)
        train_in = in_side(train_acts, in_proj, 3.5)
        pairs = []
        for idx in range(layers):
            at = scalar(idx)
            query_side, train_side = lax.psum(
                (
                    side_partial(at, query_grads, out_proj, 0.5),
                    side_partial(at, train_grads, out_proj, 1.9),
                ),
                "head",
            )
            every = lax.all_gather(ready(at, [query_side])[0], "dp", axis=0, tiled=True)
            pairs.append(([every], train_blocks(train_side, train_scale, train_in[idx : idx + 1])))
        total = lax.psum(score_terms(scalar(0), norm, pairs), "head")
    return total[:, :train_n]


def solution(mesh):
    return jax.shard_map(
        local,
        mesh=mesh,
        in_specs=(
            P(None, ("groups", "dp"), None, "head"),
            P(None, ("groups", "dp"), None, "head"),
            P(("groups", "dp"), None),
            P(None, ("groups", "dp"), None, "head"),
            P(None, ("groups", "dp"), None, "head"),
            P(("groups", "dp"), None),
            P(),
            P(None, None, "head"),
            P(None, "head", None, None),
            P(),
            P(None, "head", None, None),
        ),
        out_specs=P(None, ("groups", "dp")),
        check_vma=False,
    )
```

```python
import functools
import math

import jax
import jax.numpy as jnp
from jax import lax
from jax.experimental import pallas as pl
from jax.experimental.pallas import tpu as pltpu
from jax.sharding import PartitionSpec as P

HIGH = lax.Precision.HIGHEST
F32 = jnp.float32
BF16 = jnp.bfloat16
NT = (((1,), (1,)), ((), ()))

NEAR = [(0, 1), (1, 0), (2, 3), (3, 2)]
FAR = [(0, 2), (2, 0), (1, 3), (3, 1)]

WHOLE = pl.BlockSpec(memory_space=pltpu.VMEM)
IN_HBM = pl.BlockSpec(memory_space=pltpu.HBM)


def call(kernel, inputs, out_shape, name, *, micros, after=(), prefetch=(), grid=(1,),
         in_specs=None, out_specs=None, scratch=(), mebibytes=8):
    skip = len(prefetch) + len(inputs)

    def body(*refs):
        return kernel(*refs[:skip], *refs[skip + len(after) :])

    in_specs = in_specs or [WHOLE] * len(inputs)
    return pl.pallas_call(
        body,
        out_shape=out_shape,
        grid_spec=pltpu.PrefetchScalarGridSpec(
            num_scalar_prefetch=len(prefetch),
            grid=grid,
            in_specs=[*in_specs, *[pl.BlockSpec(memory_space=pl.ANY)] * len(after)],
            out_specs=out_specs or WHOLE,
            scratch_shapes=scratch,
        ),
        compiler_params=pltpu.CompilerParams(vmem_limit_bytes=mebibytes << 20),
        cost_estimate=pl.CostEstimate(
            flops=int(micros * 1.1e9), bytes_accessed=0, transcendentals=0
        ),
        name=name,
    )(*prefetch, *inputs, *after)


def stage(layer):
    return pl.when(layer >= 0)


def in_hbm(array):
    return pltpu.with_memory_space_constraint(array, pltpu.HBM)


def hold(array, after):
    return pl.pallas_call(
        lambda *refs: None,
        out_shape=jax.ShapeDtypeStruct(array.shape, array.dtype),
        in_specs=[WHOLE, *[pl.BlockSpec(memory_space=pl.ANY)] * len(after)],
        out_specs=WHOLE,
        input_output_aliases={0: 0},
        compiler_params=pltpu.CompilerParams(vmem_limit_bytes=1 << 20),
        cost_estimate=pl.CostEstimate(flops=0, bytes_accessed=0, transcendentals=0),
        name="hold",
    )(array, *after)


def side_kernel(layer_ref, grads_ref, proj_ref, out_ref):
    side = lax.dot_general(grads_ref[0, 0], proj_ref[0], NT, preferred_element_type=F32)
    out_ref[0] = side.T


def side_partial(layer, grads, out_proj, micros, after=()):
    _, count, length, feats = grads.shape
    rank = out_proj.shape[1]
    return call(
        side_kernel,
        [grads, out_proj],
        jax.ShapeDtypeStruct((count, rank, length), F32),
        "side_partial",
        micros=micros,
        after=after,
        prefetch=[layer],
        grid=(count,),
        in_specs=[
            pl.BlockSpec((1, 1, length, feats), lambda i, l: (l[0], i, 0, 0)),
            pl.BlockSpec((1, rank, feats), lambda i, l: (l[0], 0, 0)),
        ],
        out_specs=pl.BlockSpec((1, rank, length), lambda i, l: (i, 0, 0)),
    )


def sides_of(layer, grads_ref, proj_ref, out_ref):
    for seq in range(out_ref.shape[0]):
        out_ref[seq] = lax.dot_general(
            grads_ref[layer, seq], proj_ref[layer], NT, preferred_element_type=F32
        ).T


def sides_kernel(layer_ref, grads_ref, proj_ref, out_ref):
    sides_of(layer_ref[0], grads_ref, proj_ref, out_ref)


def sides_partial(layer, grads, out_proj, micros, after=()):
    _, count, length, feats = grads.shape
    return call(
        sides_kernel,
        [grads, out_proj],
        jax.ShapeDtypeStruct((count, out_proj.shape[1], length), F32),
        "sides_partial",
        micros=micros,
        after=after,
        prefetch=[layer],
        mebibytes=4,
    )


def both_kernel(
    layer_ref, ids_ref, acts_ref, in_proj_ref, table_ref, grads_ref, proj_ref,
    in_ref, scale_ref, out_ref,
):
    for at in range(acts_ref.shape[0]):
        for seq in range(acts_ref.shape[1]):
            in_side_of(acts_ref.at[at, seq], in_proj_ref.at[at], in_ref, (at, seq))
    token_kernel(ids_ref, table_ref, scale_ref)
    sides_of(layer_ref[0], grads_ref, proj_ref, out_ref)


def query_in_and_side(
    layer, ids, acts, in_proj, token_weight, grads, out_proj, micros, after=()
):
    layers, acts_n, length, feats = acts.shape
    _, heads, rank, width = in_proj.shape
    count = grads.shape[1]
    return call(
        both_kernel,
        [ids, acts, in_proj, token_table(token_weight), grads, out_proj],
        [
            jax.ShapeDtypeStruct((layers, acts_n, length, heads * rank), BF16),
            jax.ShapeDtypeStruct(ids.shape, F32),
            jax.ShapeDtypeStruct((count, rank, length), F32),
        ],
        "query_in_and_side",
        micros=micros,
        after=after,
        mebibytes=8,
        prefetch=[layer],
        out_specs=[WHOLE] * 3,
    )


def first_kernel(layer_ref, grads_hbm, proj_hbm, out_ref, grads, proj, sems):
    layer = layer_ref[0]
    copies = [
        pltpu.make_async_copy(proj_hbm.at[layer], proj, sems.at[0]),
        pltpu.make_async_copy(grads_hbm.at[layer], grads, sems.at[1]),
    ]
    for copy in copies:
        copy.start()
    for copy in copies:
        copy.wait()

    @stage(layer)
    def _():
        for seq in range(grads.shape[0]):
            out_ref[seq] = lax.dot_general(
                grads[seq], proj[...], NT, preferred_element_type=F32
            ).T


def first_partial(layer, grads, out_proj, micros):
    _, count, length, feats = grads.shape
    rank = out_proj.shape[1]
    return call(
        first_kernel,
        [in_hbm(grads), in_hbm(out_proj)],
        jax.ShapeDtypeStruct((count, rank, length), F32),
        "first_partial",
        micros=micros,
        prefetch=[layer],
        in_specs=[IN_HBM, IN_HBM],
        scratch=[
            pltpu.VMEM((count, length, feats), BF16),
            pltpu.VMEM((rank, feats), BF16),
            pltpu.SemaphoreType.DMA((2,)),
        ],
    )


def in_side_of(acts, proj, out_ref, at):
    heads, rank, width = proj.shape
    none = jnp.zeros((rank, width), BF16)
    for pair in range(heads // 2):
        one, two = proj[2 * pair], proj[2 * pair + 1]
        both = jnp.concatenate(
            [jnp.concatenate([one, none], axis=1), jnp.concatenate([none, two], axis=1)], axis=0
        )
        pair_acts = acts[:, 2 * width * pair : 2 * width * (pair + 1)]
        side = lax.dot_general(pair_acts, both, NT, preferred_element_type=F32)
        out_ref[(*at, slice(None), slice(2 * rank * pair, 2 * rank * (pair + 1)))] = side.astype(
            BF16
        )


def in_kernel(acts_ref, proj_ref, out_ref):
    in_side_of(acts_ref.at[0, 0], proj_ref.at[0], out_ref, (0, 0))


def in_side(acts, in_proj, micros, after=()):
    layers, count, length, feats = acts.shape
    _, heads, rank, width = in_proj.shape
    return call(
        in_kernel,
        [acts, in_proj],
        jax.ShapeDtypeStruct((layers, count, length, heads * rank), BF16),
        "in_side",
        micros=micros,
        after=after,
        grid=(layers, count),
        in_specs=[
            pl.BlockSpec((1, 1, length, feats), lambda l, i: (l, i, 0, 0)),
            pl.BlockSpec((1, heads, rank, width), lambda l, i: (l, 0, 0, 0)),
        ],
        out_specs=pl.BlockSpec((1, 1, length, heads * rank), lambda l, i: (l, i, 0, 0)),
    )


def streamed_kernel(layer_ref, acts_hbm, proj_ref, one_ref, two_ref, acts, sems):
    layers, count = acts.shape[:2]
    order = [layer_ref[0], 1 - layer_ref[0]]
    steps = [(layer, seq) for layer in range(layers) for seq in range(count)]

    def copy(step):
        layer, seq = steps[step]
        return pltpu.make_async_copy(
            acts_hbm.at[order[layer], seq], acts.at[layer, seq], sems.at[step]
        )

    for step in range(len(steps)):
        copy(step).start()
    for step, (layer, seq) in enumerate(steps):
        copy(step).wait()

        @stage(layer_ref[0])
        def _():
            in_side_of(
                acts.at[layer, seq], proj_ref.at[order[layer]], (one_ref, two_ref)[layer], (seq,)
            )


def in_side_streamed(layer, acts, in_proj, micros, after=()):
    layers, count, length, feats = acts.shape
    _, heads, rank, width = in_proj.shape
    return call(
        streamed_kernel,
        [in_hbm(acts), in_proj],
        [jax.ShapeDtypeStruct((count, length, heads * rank), BF16)] * 2,
        "in_side_streamed",
        micros=micros,
        mebibytes=20,
        prefetch=[layer],
        after=after,
        in_specs=[IN_HBM, WHOLE],
        out_specs=[WHOLE] * 2,
        scratch=[
            pltpu.VMEM(acts.shape, BF16),
            pltpu.SemaphoreType.DMA((layers * count,)),
        ],
    )


def settle_kernel(one_ref, two_ref, out_ref):
    out_ref[...] = one_ref[...] + two_ref[...]


def settle(one, two, after):
    return call(
        settle_kernel, [one, two], jax.ShapeDtypeStruct(one.shape, F32), "settle", micros=0.1,
        after=after,
    )


def token_kernel(ids_ref, table_ref, out_ref):
    table = table_ref[...]
    rows, lanes = table.shape
    high = table.astype(BF16)
    rest = table - high.astype(F32)
    mid = rest.astype(BF16)
    low = (rest - mid.astype(F32)).astype(BF16)
    turned = [part.T for part in (high, mid, low)]
    length = ids_ref.shape[1]
    for row in range(ids_ref.shape[0]):
        ids = ids_ref[row : row + 1, :]
        block = ids // lanes
        at = lax.broadcasted_iota(jnp.int32, (rows, length), 0) == block
        hot = jnp.where(at, 1.0, 0.0).astype(BF16)
        picked = sum(jnp.dot(part, hot, preferred_element_type=F32) for part in turned)
        lane = lax.broadcasted_iota(jnp.int32, (lanes, length), 0) == ids - block * lanes
        out_ref[row : row + 1, :] = jnp.sum(
            jnp.where(lane, picked, 0.0), axis=0, keepdims=True
        )


def token_table(token_weight):
    lanes = 128
    return jnp.pad(token_weight, (0, -token_weight.shape[0] % lanes)).reshape(-1, lanes)


def token_scale(ids, token_weight, micros, after=()):
    table = token_table(token_weight)
    return call(
        token_kernel,
        [ids, table],
        jax.ShapeDtypeStruct(ids.shape, F32),
        "token_scale",
        micros=micros,
        after=after,
    )


def blocks_of(side, scale, in_side_seq):
    weighted = (side * scale).astype(BF16)
    product = jnp.dot(weighted, in_side_seq, preferred_element_type=F32)
    return product * (1.0 / math.sqrt(side.shape[1]))


def ready_kernel(layer_ref, own_ref, other_ref, scale_ref, in_ref, *refs):
    out_factor_ref, in_factor_ref, *out_refs = refs
    layers, heads, rank, _ = in_factor_ref.shape
    none = jnp.zeros((rank, rank), F32)
    for layer in range(layers):
        lefts = []
        for seq in range(out_refs[layer].shape[0]):
            side = jnp.where(layer_ref[0] == layer, own_ref[seq], other_ref[seq])
            blocks = blocks_of(side, scale_ref[seq : seq + 1, :], in_ref[layer, seq])
            lefts.append(
                jnp.dot(out_factor_ref[layer], blocks, precision=HIGH, preferred_element_type=F32)
            )
        for pair in range(heads // 2):
            one, two = in_factor_ref[layer, 2 * pair], in_factor_ref[layer, 2 * pair + 1]
            both = jnp.concatenate(
                [jnp.concatenate([one, none], axis=1), jnp.concatenate([none, two], axis=1)],
                axis=0,
            )
            span = slice(2 * rank * pair, 2 * rank * (pair + 1))
            for seq, left in enumerate(lefts):
                out_refs[layer][seq, :, span] = jnp.dot(
                    left[:, span], both, precision=HIGH, preferred_element_type=F32
                )


def query_ready(layer, own, other, scale, in_sides, out_factor, in_factor, after=()):
    layers, count, _, wide = in_sides.shape
    rank = own.shape[1]
    return call(
        ready_kernel,
        [own, other, scale, in_sides, out_factor, in_factor],
        [jax.ShapeDtypeStruct((count, rank, wide), F32)] * layers,
        "query_ready",
        micros=0.1,
        prefetch=[layer],
        after=after,
        out_specs=[WHOLE] * layers,
    )


def score_kernel(layers, queries_n, sides_n, first, norm, at_ref, *refs):
    query_refs, refs = refs[:queries_n], refs[queries_n:]
    side_refs, refs = refs[:sides_n], refs[sides_n:]
    scale_ref, in_ref, *before_refs, out_ref = refs
    rows, lanes = out_ref.shape
    row_at = lax.broadcasted_iota(jnp.int32, (rows, lanes), 0)
    lane_at = lax.broadcasted_iota(jnp.int32, (rows, lanes), 1)
    total = jnp.zeros((rows, lanes), F32)
    for ref in before_refs:
        total = total + ref[...]
    queries = [(refs, idx) for refs in zip(*[iter(query_refs)] * layers) for idx in range(refs[0].shape[0])]
    sides = [(ref, idx) for ref in side_refs for idx in range(ref.shape[0])]
    for seq, (side_ref, side_idx) in enumerate(sides, first):
        blocks = blocks_of(side_ref[side_idx], scale_ref[seq : seq + 1, :], in_ref[seq])
        for row, (layer_refs, idx) in enumerate(queries):
            query = layer_refs[0][idx]
            for layer in range(1, layers):
                query = jnp.where(at_ref[0] == layer, layer_refs[layer][idx], query)
            product = jnp.sum(query * blocks, axis=0, keepdims=True)
            value = jnp.sum(product, axis=1, keepdims=True) * norm
            here = (row_at == (row ^ at_ref[1])) & (lane_at == seq)
            total = total + jnp.where(here, value, 0.0)
    out_ref[...] = total


def score_terms(layer, flip, norm, queries, sides, scale, in_sides, before=(), first=0, micros=1.5):
    layers = len(queries[0])
    rows = sum(query[0].shape[0] for query in queries)
    flat = [array for query in queries for array in query]
    return call(
        functools.partial(score_kernel, layers, len(flat), len(sides), first, norm),
        [*flat, *sides, scale, in_sides, *before],
        jax.ShapeDtypeStruct((rows, 128), F32),
        "score_terms",
        micros=micros,
        prefetch=[jnp.concatenate([layer, flip])],
    )


def local(
    train_grads,
    train_acts,
    train_ids,
    query_grads,
    query_acts,
    query_ids,
    token_weight,
    out_proj,
    in_proj,
    out_factor,
    in_factor,
):
    layers, train_n = train_grads.shape[:2]
    query_n = query_ids.shape[0]
    heads, rank = in_proj.shape[1:3]
    n_head, n_dp = lax.axis_size("head"), lax.axis_size("dp")
    by_pairs = n_head == 4 and n_dp == 4 and layers == 2 and query_n == 1
    norm = 1.0 / math.sqrt(layers * heads * n_head * rank * rank)

    def scalar(idx):
        return jnp.asarray(idx, jnp.int32).reshape(1)

    def near(array, axis="head"):
        return lax.ppermute(array, axis, NEAR)

    def far(array, axis="head"):
        return lax.ppermute(array, axis, FAR)

    if by_pairs:
        mine = scalar(lax.axis_index("head") % 2)
        other = 1 - mine
        flip = scalar(lax.axis_index("dp"))
        query_out = first_partial(other, query_grads, out_proj, 8.0)
        query_got = near(query_out)
        train_out = sides_partial(other, train_grads, out_proj, 2.0, [query_out])
        query_keep = sides_partial(mine, query_grads, out_proj, 0.5, [train_out])
        query_pair = query_keep + query_got
        query_far = far(query_pair)
        train_got = near(train_out)
        query_in, query_scale, train_keep = query_in_and_side(
            mine, query_ids, query_acts, in_proj, token_weight, train_grads, out_proj, 3.0,
            [query_pair],
        )
        query_own = settle(query_pair, query_far, [query_scale])
        query_other = near(query_own)
        parts = [(i * train_n // 1, (i + 1) * train_n // 1) for i in range(1)]
        pairs = [train_keep[a:b] + train_got[a:b] for a, b in parts]
        ready = query_ready(
            mine, query_own, query_other, query_scale, query_in, out_factor, in_factor, pairs
        )
        across = [far(one, "dp") for one in ready]
        train_scale = token_scale(train_ids, token_weight, 0.1, ready[-1:])
        owns = [pair + far(pair) for pair in pairs]
        others = [near(own) for own in owns]
        across = [hold(one, owns[-1:]) for one in across]
        every = [
            ready,
            [near(one, "dp") for one in ready],
            across,
            [near(one, "dp") for one in across],
        ]
        in_own, in_other = in_side_streamed(mine, train_acts, in_proj, 5.0, owns)
        terms = score_terms(mine, flip, norm, every, owns, train_scale, in_own)
        for (first, _), part in zip(parts, others):
            terms = score_terms(
                other, flip, norm, every, [part], train_scale, in_other, [terms], first
            )
        total = terms
        for shift in range(1, 4):
            total = total + lax.ppermute(
                terms, "head", [(idx, (idx + shift) % 4) for idx in range(4)]
            )
    else:
        query_scale = token_scale(query_ids, token_weight, 0.5)
        train_scale = token_scale(train_ids, token_weight, 1.5)
        query_in = in_side(query_acts, in_proj, 0.9)
        train_in = in_side(train_acts, in_proj, 3.5)
        at = [scalar(idx) for idx in range(layers)]
        query_sides, train_sides = lax.psum(
            (
                [side_partial(idx, query_grads, out_proj, 0.5) for idx in at],
                [side_partial(idx, train_grads, out_proj, 1.9) for idx in at],
            ),
            "head",
        )
        ready = query_ready(
            at[0], *query_sides, query_scale, query_in, out_factor, in_factor
        )
        every = [[lax.all_gather(one, "dp", axis=0, tiled=True) for one in ready]]
        terms = []
        for layer, idx in enumerate(at):
            sides, in_sides = train_sides[layer], train_in[layer]
            before = terms[-1:]
            terms.append(
                score_terms(idx, scalar(0), norm, every, [sides], train_scale, in_sides, before)
            )
        total = lax.psum(terms[-1], "head")
    return total[:, :train_n]


def solution(mesh):
    return jax.shard_map(
        local,
        mesh=mesh,
        in_specs=(
            P(None, ("groups", "dp"), None, "head"),
            P(None, ("groups", "dp"), None, "head"),
            P(("groups", "dp"), None),
            P(None, ("groups", "dp"), None, "head"),
            P(None, ("groups", "dp"), None, "head"),
            P(("groups", "dp"), None),
            P(),
            P(None, None, "head"),
            P(None, "head", None, None),
            P(),
            P(None, "head", None, None),
        ),
        out_specs=P(None, ("groups", "dp")),
        check_vma=False,
    )
```

```python
import functools
import math

import jax
import jax.numpy as jnp
from jax import lax
from jax.experimental import pallas as pl
from jax.experimental.pallas import tpu as pltpu
from jax.sharding import PartitionSpec as P

HIGH = lax.Precision.HIGHEST
F32 = jnp.float32
BF16 = jnp.bfloat16
NT = (((1,), (1,)), ((), ()))

NEAR = [(0, 1), (1, 0), (2, 3), (3, 2)]
FAR = [(0, 2), (2, 0), (1, 3), (3, 1)]

WHOLE = pl.BlockSpec(memory_space=pltpu.VMEM)
IN_HBM = pl.BlockSpec(memory_space=pltpu.HBM)


def call(kernel, inputs, out_shape, name, *, micros, after=(), prefetch=(), grid=(1,),
         in_specs=None, out_specs=None, scratch=(), mebibytes=8):
    skip = len(prefetch) + len(inputs)

    def body(*refs):
        return kernel(*refs[:skip], *refs[skip + len(after) :])

    in_specs = in_specs or [WHOLE] * len(inputs)
    return pl.pallas_call(
        body,
        out_shape=out_shape,
        grid_spec=pltpu.PrefetchScalarGridSpec(
            num_scalar_prefetch=len(prefetch),
            grid=grid,
            in_specs=[*in_specs, *[pl.BlockSpec(memory_space=pl.ANY)] * len(after)],
            out_specs=out_specs or WHOLE,
            scratch_shapes=scratch,
        ),
        compiler_params=pltpu.CompilerParams(vmem_limit_bytes=mebibytes << 20),
        cost_estimate=pl.CostEstimate(
            flops=int(micros * 1.1e9), bytes_accessed=0, transcendentals=0
        ),
        name=name,
    )(*prefetch, *inputs, *after)


def stage(layer):
    return pl.when(layer >= 0)


def in_hbm(array):
    return pltpu.with_memory_space_constraint(array, pltpu.HBM)


def hold(array, after):
    return pl.pallas_call(
        lambda *refs: None,
        out_shape=jax.ShapeDtypeStruct(array.shape, array.dtype),
        in_specs=[WHOLE, *[pl.BlockSpec(memory_space=pl.ANY)] * len(after)],
        out_specs=WHOLE,
        input_output_aliases={0: 0},
        compiler_params=pltpu.CompilerParams(vmem_limit_bytes=1 << 20),
        cost_estimate=pl.CostEstimate(flops=0, bytes_accessed=0, transcendentals=0),
        name="hold",
    )(array, *after)


def side_kernel(layer_ref, grads_ref, proj_ref, out_ref):
    side = lax.dot_general(grads_ref[0, 0], proj_ref[0], NT, preferred_element_type=F32)
    out_ref[0] = side.T


def side_partial(layer, grads, out_proj, micros, after=()):
    _, count, length, feats = grads.shape
    rank = out_proj.shape[1]
    return call(
        side_kernel,
        [grads, out_proj],
        jax.ShapeDtypeStruct((count, rank, length), F32),
        "side_partial",
        micros=micros,
        after=after,
        prefetch=[layer],
        grid=(count,),
        in_specs=[
            pl.BlockSpec((1, 1, length, feats), lambda i, l: (l[0], i, 0, 0)),
            pl.BlockSpec((1, rank, feats), lambda i, l: (l[0], 0, 0)),
        ],
        out_specs=pl.BlockSpec((1, rank, length), lambda i, l: (i, 0, 0)),
    )


def sides_of(layer, grads_ref, proj_ref, out_ref):
    for seq in range(out_ref.shape[0]):
        out_ref[seq] = lax.dot_general(
            grads_ref[layer, seq], proj_ref[layer], NT, preferred_element_type=F32
        ).T


def sides_kernel(layer_ref, grads_ref, proj_ref, out_ref):
    sides_of(layer_ref[0], grads_ref, proj_ref, out_ref)


def sides_partial(layer, grads, out_proj, micros, after=()):
    _, count, length, feats = grads.shape
    return call(
        sides_kernel,
        [grads, out_proj],
        jax.ShapeDtypeStruct((count, out_proj.shape[1], length), F32),
        "sides_partial",
        micros=micros,
        after=after,
        prefetch=[layer],
        mebibytes=4,
    )


def both_kernel(
    layer_ref, ids_ref, acts_ref, in_proj_ref, table_ref, grads_ref, proj_ref,
    in_ref, scale_ref, out_ref,
):
    for at in range(acts_ref.shape[0]):
        for seq in range(acts_ref.shape[1]):
            in_side_of(acts_ref.at[at, seq], in_proj_ref.at[at], in_ref, (at, seq))
    token_kernel(ids_ref, table_ref, scale_ref)
    sides_of(layer_ref[0], grads_ref, proj_ref, out_ref)


def query_in_and_side(
    layer, ids, acts, in_proj, token_weight, grads, out_proj, micros, after=()
):
    layers, acts_n, length, feats = acts.shape
    _, heads, rank, width = in_proj.shape
    count = grads.shape[1]
    return call(
        both_kernel,
        [ids, acts, in_proj, token_table(token_weight), grads, out_proj],
        [
            jax.ShapeDtypeStruct((layers, acts_n, length, heads * rank), BF16),
            jax.ShapeDtypeStruct(ids.shape, F32),
            jax.ShapeDtypeStruct((count, rank, length), F32),
        ],
        "query_in_and_side",
        micros=micros,
        after=after,
        mebibytes=8,
        prefetch=[layer],
        out_specs=[WHOLE] * 3,
    )


def first_kernel(layer_ref, grads_hbm, proj_hbm, out_ref, grads, proj, sems):
    layer = layer_ref[0]
    copies = [
        pltpu.make_async_copy(proj_hbm.at[layer], proj, sems.at[0]),
        pltpu.make_async_copy(grads_hbm.at[layer], grads, sems.at[1]),
    ]
    for copy in copies:
        copy.start()
    for copy in copies:
        copy.wait()

    @stage(layer)
    def _():
        for seq in range(grads.shape[0]):
            out_ref[seq] = lax.dot_general(
                grads[seq], proj[...], NT, preferred_element_type=F32
            ).T


def first_partial(layer, grads, out_proj, micros):
    _, count, length, feats = grads.shape
    rank = out_proj.shape[1]
    return call(
        first_kernel,
        [in_hbm(grads), in_hbm(out_proj)],
        jax.ShapeDtypeStruct((count, rank, length), F32),
        "first_partial",
        micros=micros,
        prefetch=[layer],
        in_specs=[IN_HBM, IN_HBM],
        scratch=[
            pltpu.VMEM((count, length, feats), BF16),
            pltpu.VMEM((rank, feats), BF16),
            pltpu.SemaphoreType.DMA((2,)),
        ],
    )


def in_side_of(acts, proj, out_ref, at):
    heads, rank, width = proj.shape
    none = jnp.zeros((rank, width), BF16)
    for pair in range(heads // 2):
        one, two = proj[2 * pair], proj[2 * pair + 1]
        both = jnp.concatenate(
            [jnp.concatenate([one, none], axis=1), jnp.concatenate([none, two], axis=1)], axis=0
        )
        pair_acts = acts[:, 2 * width * pair : 2 * width * (pair + 1)]
        side = lax.dot_general(pair_acts, both, NT, preferred_element_type=F32)
        out_ref[(*at, slice(None), slice(2 * rank * pair, 2 * rank * (pair + 1)))] = side.astype(
            BF16
        )


def in_kernel(acts_ref, proj_ref, out_ref):
    in_side_of(acts_ref.at[0, 0], proj_ref.at[0], out_ref, (0, 0))


def in_side(acts, in_proj, micros, after=()):
    layers, count, length, feats = acts.shape
    _, heads, rank, width = in_proj.shape
    return call(
        in_kernel,
        [acts, in_proj],
        jax.ShapeDtypeStruct((layers, count, length, heads * rank), BF16),
        "in_side",
        micros=micros,
        after=after,
        grid=(layers, count),
        in_specs=[
            pl.BlockSpec((1, 1, length, feats), lambda l, i: (l, i, 0, 0)),
            pl.BlockSpec((1, heads, rank, width), lambda l, i: (l, 0, 0, 0)),
        ],
        out_specs=pl.BlockSpec((1, 1, length, heads * rank), lambda l, i: (l, i, 0, 0)),
    )


def layer_in_kernel(layer_ref, acts_ref, proj_ref, out_ref):
    layer = layer_ref[0]
    for seq in range(out_ref.shape[0]):
        in_side_of(acts_ref.at[layer, seq], proj_ref.at[layer], out_ref, (seq,))


def in_side_of_layer(layer, acts, in_proj, micros, after=()):
    _, count, length, _ = acts.shape
    _, heads, rank, _ = in_proj.shape
    return call(
        layer_in_kernel,
        [acts, in_proj],
        jax.ShapeDtypeStruct((count, length, heads * rank), BF16),
        "in_side_of_layer",
        micros=micros,
        prefetch=[layer],
        after=after,
    )


def stage_kernel(acts_hbm, out_ref, tick_ref, sems):
    layers, count = out_ref.shape[:2]
    copies = [
        pltpu.make_async_copy(
            acts_hbm.at[layer, seq], out_ref.at[layer, seq], sems.at[layer * count + seq]
        )
        for layer in range(layers)
        for seq in range(count)
    ]
    for copy in copies:
        copy.start()
    tick_ref[...] = jnp.zeros_like(tick_ref)
    for copy in copies:
        copy.wait()


def staged(acts, after):
    return call(
        stage_kernel,
        [in_hbm(acts)],
        [jax.ShapeDtypeStruct(acts.shape, BF16), jax.ShapeDtypeStruct((8, 128), F32)],
        "staged",
        micros=0.1,
        after=after,
        in_specs=[IN_HBM],
        out_specs=[WHOLE] * 2,
        scratch=[pltpu.SemaphoreType.DMA((acts.shape[0] * acts.shape[1],))],
    )


def settle_kernel(one_ref, two_ref, out_ref):
    out_ref[...] = one_ref[...] + two_ref[...]


def settle(one, two, after):
    return call(
        settle_kernel, [one, two], jax.ShapeDtypeStruct(one.shape, F32), "settle", micros=0.1,
        after=after,
    )


def token_kernel(ids_ref, table_ref, out_ref):
    table = table_ref[...]
    rows, lanes = table.shape
    high = table.astype(BF16)
    rest = table - high.astype(F32)
    mid = rest.astype(BF16)
    low = (rest - mid.astype(F32)).astype(BF16)
    turned = [part.T for part in (high, mid, low)]
    length = ids_ref.shape[1]
    for row in range(ids_ref.shape[0]):
        ids = ids_ref[row : row + 1, :]
        block = ids // lanes
        at = lax.broadcasted_iota(jnp.int32, (rows, length), 0) == block
        hot = jnp.where(at, 1.0, 0.0).astype(BF16)
        picked = sum(jnp.dot(part, hot, preferred_element_type=F32) for part in turned)
        lane = lax.broadcasted_iota(jnp.int32, (lanes, length), 0) == ids - block * lanes
        out_ref[row : row + 1, :] = jnp.sum(
            jnp.where(lane, picked, 0.0), axis=0, keepdims=True
        )


def token_table(token_weight):
    lanes = 128
    return jnp.pad(token_weight, (0, -token_weight.shape[0] % lanes)).reshape(-1, lanes)


def token_scale(ids, token_weight, micros, after=()):
    table = token_table(token_weight)
    return call(
        token_kernel,
        [ids, table],
        jax.ShapeDtypeStruct(ids.shape, F32),
        "token_scale",
        micros=micros,
        after=after,
    )


def blocks_of(side, scale, in_side_seq):
    weighted = (side * scale).astype(BF16)
    product = jnp.dot(weighted, in_side_seq, preferred_element_type=F32)
    return product * (1.0 / math.sqrt(side.shape[1]))


def ready_kernel(layer_ref, own_ref, other_ref, scale_ref, in_ref, *refs):
    out_factor_ref, in_factor_ref, *out_refs = refs
    layers, heads, rank, _ = in_factor_ref.shape
    none = jnp.zeros((rank, rank), F32)
    for layer in range(layers):
        lefts = []
        for seq in range(out_refs[layer].shape[0]):
            side = jnp.where(layer_ref[0] == layer, own_ref[seq], other_ref[seq])
            blocks = blocks_of(side, scale_ref[seq : seq + 1, :], in_ref[layer, seq])
            lefts.append(
                jnp.dot(out_factor_ref[layer], blocks, precision=HIGH, preferred_element_type=F32)
            )
        for pair in range(heads // 2):
            one, two = in_factor_ref[layer, 2 * pair], in_factor_ref[layer, 2 * pair + 1]
            both = jnp.concatenate(
                [jnp.concatenate([one, none], axis=1), jnp.concatenate([none, two], axis=1)],
                axis=0,
            )
            span = slice(2 * rank * pair, 2 * rank * (pair + 1))
            for seq, left in enumerate(lefts):
                out_refs[layer][seq, :, span] = jnp.dot(
                    left[:, span], both, precision=HIGH, preferred_element_type=F32
                )


def query_ready(layer, own, other, scale, in_sides, out_factor, in_factor, after=()):
    layers, count, _, wide = in_sides.shape
    rank = own.shape[1]
    return call(
        ready_kernel,
        [own, other, scale, in_sides, out_factor, in_factor],
        [jax.ShapeDtypeStruct((count, rank, wide), F32)] * layers,
        "query_ready",
        micros=0.1,
        prefetch=[layer],
        after=after,
        out_specs=[WHOLE] * layers,
    )


def score_kernel(layers, queries_n, sides_n, first, norm, at_ref, *refs):
    query_refs, refs = refs[:queries_n], refs[queries_n:]
    side_refs, refs = refs[:sides_n], refs[sides_n:]
    scale_ref, in_ref, *before_refs, out_ref = refs
    rows, lanes = out_ref.shape
    row_at = lax.broadcasted_iota(jnp.int32, (rows, lanes), 0)
    lane_at = lax.broadcasted_iota(jnp.int32, (rows, lanes), 1)
    total = jnp.zeros((rows, lanes), F32)
    for ref in before_refs:
        total = total + ref[...]
    queries = [(refs, idx) for refs in zip(*[iter(query_refs)] * layers) for idx in range(refs[0].shape[0])]
    sides = [(ref, idx) for ref in side_refs for idx in range(ref.shape[0])]
    for seq, (side_ref, side_idx) in enumerate(sides, first):
        blocks = blocks_of(side_ref[side_idx], scale_ref[seq : seq + 1, :], in_ref[seq])
        for row, (layer_refs, idx) in enumerate(queries):
            query = layer_refs[0][idx]
            for layer in range(1, layers):
                query = jnp.where(at_ref[0] == layer, layer_refs[layer][idx], query)
            product = jnp.sum(query * blocks, axis=0, keepdims=True)
            value = jnp.sum(product, axis=1, keepdims=True) * norm
            here = (row_at == (row ^ at_ref[1])) & (lane_at == seq)
            total = total + jnp.where(here, value, 0.0)
    out_ref[...] = total


def score_terms(layer, flip, norm, queries, sides, scale, in_sides, before=(), first=0, micros=1.5):
    layers = len(queries[0])
    rows = sum(query[0].shape[0] for query in queries)
    flat = [array for query in queries for array in query]
    return call(
        functools.partial(score_kernel, layers, len(flat), len(sides), first, norm),
        [*flat, *sides, scale, in_sides, *before],
        jax.ShapeDtypeStruct((rows, 128), F32),
        "score_terms",
        micros=micros,
        prefetch=[jnp.concatenate([layer, flip])],
    )


def lever_kernel(layers, queries_n, layer_ref, *refs):
    query_refs, (in_ref, out_ref) = refs[:queries_n], refs[queries_n:]
    rows = []
    for layer_refs in zip(*[iter(query_refs)] * layers):
        for idx in range(layer_refs[0].shape[0]):
            query = layer_refs[0][idx]
            for layer in range(1, layers):
                query = jnp.where(layer_ref[0] == layer, layer_refs[layer][idx], query)
            rows.append(query.astype(BF16))
    stacked = jnp.concatenate(rows, axis=0)
    for seq in range(in_ref.shape[0]):
        out_ref[seq] = lax.dot_general(stacked, in_ref[seq], NT, preferred_element_type=F32)


def query_levers(layer, queries, in_sides):
    flat = [array for query in queries for array in query]
    rows = sum(query[0].shape[0] * query[0].shape[1] for query in queries)
    count, length, _ = in_sides.shape
    return call(
        functools.partial(lever_kernel, len(queries[0]), len(flat)),
        [*flat, in_sides],
        jax.ShapeDtypeStruct((count, rows, length), F32),
        "query_levers",
        micros=1.5,
        prefetch=[layer],
    )


def lever_score_kernel(norm, flip_ref, lever_ref, side_ref, scale_ref, before_ref, out_ref):
    rows, lanes = out_ref.shape
    rank = side_ref.shape[1]
    row_at = lax.broadcasted_iota(jnp.int32, (rows, lanes), 0)
    lane_at = lax.broadcasted_iota(jnp.int32, (rows, lanes), 1)
    total = before_ref[...]
    for seq in range(side_ref.shape[0]):
        weighted = (side_ref[seq] * scale_ref[seq : seq + 1, :]).astype(BF16).astype(F32)
        for row in range(rows):
            product = lever_ref[seq, rank * row : rank * (row + 1), :] * weighted
            value = jnp.sum(jnp.sum(product, axis=0, keepdims=True), axis=1, keepdims=True)
            here = (row_at == (row ^ flip_ref[0])) & (lane_at == seq)
            total = total + jnp.where(here, value * norm, 0.0)
    out_ref[...] = total


def lever_scores(flip, norm, levers, side, scale, before):
    return call(
        functools.partial(lever_score_kernel, norm / math.sqrt(side.shape[2])),
        [levers, side, scale, before],
        jax.ShapeDtypeStruct(before.shape, F32),
        "lever_scores",
        micros=0.5,
        prefetch=[flip],
    )


def local(
    train_grads,
    train_acts,
    train_ids,
    query_grads,
    query_acts,
    query_ids,
    token_weight,
    out_proj,
    in_proj,
    out_factor,
    in_factor,
):
    layers, train_n = train_grads.shape[:2]
    query_n = query_ids.shape[0]
    heads, rank = in_proj.shape[1:3]
    n_head, n_dp = lax.axis_size("head"), lax.axis_size("dp")
    by_pairs = n_head == 4 and n_dp == 4 and layers == 2 and query_n == 1
    norm = 1.0 / math.sqrt(layers * heads * n_head * rank * rank)

    def scalar(idx):
        return jnp.asarray(idx, jnp.int32).reshape(1)

    def near(array, axis="head"):
        return lax.ppermute(array, axis, NEAR)

    def far(array, axis="head"):
        return lax.ppermute(array, axis, FAR)

    if by_pairs:
        mine = scalar(lax.axis_index("head") % 2)
        other = 1 - mine
        flip = scalar(lax.axis_index("dp"))
        query_out = first_partial(other, query_grads, out_proj, 8.0)
        query_got = near(query_out)
        train_out = sides_partial(other, train_grads, out_proj, 2.0, [query_out])
        query_keep = sides_partial(mine, query_grads, out_proj, 0.5, [train_out])
        query_pair = query_keep + query_got
        query_far = far(query_pair)
        train_got = near(train_out)
        query_in, query_scale, train_keep = query_in_and_side(
            mine, query_ids, query_acts, in_proj, token_weight, train_grads, out_proj, 3.0,
            [query_pair],
        )
        query_own = settle(query_pair, query_far, [query_scale])
        query_other = near(query_own)
        parts = [(i * train_n // 1, (i + 1) * train_n // 1) for i in range(1)]
        pairs = [train_keep[a:b] + train_got[a:b] for a, b in parts]
        ready = query_ready(
            mine, query_own, query_other, query_scale, query_in, out_factor, in_factor, pairs
        )
        across = [far(one, "dp") for one in ready]
        train_scale = token_scale(train_ids, token_weight, 0.1, ready[-1:])
        acts, tick = staged(train_acts, [train_scale])
        owns = [pair + hold(far(pair), [tick]) for pair in pairs]
        others = [near(own) for own in owns]
        in_other = in_side_of_layer(other, acts, in_proj, 2.5, owns)
        across = [hold(across[0], [owns[0]]), hold(across[1], [owns[0]])]
        in_own = in_side_of_layer(mine, acts, in_proj, 6.0, [in_other])
        every = [
            ready,
            [near(one, "dp") for one in ready],
            across,
            [near(one, "dp") for one in across],
        ]
        terms = score_terms(mine, flip, norm, every, owns, train_scale, in_own)
        levers = query_levers(other, every, in_other)
        terms = lever_scores(flip, norm, levers, others[0], train_scale, terms)
        total = terms
        for shift in range(1, 4):
            total = total + lax.ppermute(
                terms, "head", [(idx, (idx + shift) % 4) for idx in range(4)]
            )
    else:
        query_scale = token_scale(query_ids, token_weight, 0.5)
        train_scale = token_scale(train_ids, token_weight, 1.5)
        query_in = in_side(query_acts, in_proj, 0.9)
        train_in = in_side(train_acts, in_proj, 3.5)
        at = [scalar(idx) for idx in range(layers)]
        query_sides, train_sides = lax.psum(
            (
                [side_partial(idx, query_grads, out_proj, 0.5) for idx in at],
                [side_partial(idx, train_grads, out_proj, 1.9) for idx in at],
            ),
            "head",
        )
        ready = query_ready(
            at[0], *query_sides, query_scale, query_in, out_factor, in_factor
        )
        every = [[lax.all_gather(one, "dp", axis=0, tiled=True) for one in ready]]
        terms = []
        for layer, idx in enumerate(at):
            sides, in_sides = train_sides[layer], train_in[layer]
            before = terms[-1:]
            terms.append(
                score_terms(idx, scalar(0), norm, every, [sides], train_scale, in_sides, before)
            )
        total = lax.psum(terms[-1], "head")
    return total[:, :train_n]


def solution(mesh):
    return jax.shard_map(
        local,
        mesh=mesh,
        in_specs=(
            P(None, ("groups", "dp"), None, "head"),
            P(None, ("groups", "dp"), None, "head"),
            P(("groups", "dp"), None),
            P(None, ("groups", "dp"), None, "head"),
            P(None, ("groups", "dp"), None, "head"),
            P(("groups", "dp"), None),
            P(),
            P(None, None, "head"),
            P(None, "head", None, None),
            P(),
            P(None, "head", None, None),
        ),
        out_specs=P(None, ("groups", "dp")),
        check_vma=False,
    )
```

```python
import functools
import math

import jax
import jax.numpy as jnp
from jax import lax
from jax.experimental import pallas as pl
from jax.experimental.pallas import tpu as pltpu
from jax.sharding import PartitionSpec as P

HIGH = lax.Precision.HIGHEST
F32 = jnp.float32
BF16 = jnp.bfloat16
NT = (((1,), (1,)), ((), ()))

NEAR = [(0, 1), (1, 0), (2, 3), (3, 2)]
FAR = [(0, 2), (2, 0), (1, 3), (3, 1)]

WHOLE = pl.BlockSpec(memory_space=pltpu.VMEM)
IN_HBM = pl.BlockSpec(memory_space=pltpu.HBM)


def call(kernel, inputs, out_shape, name, *, micros, after=(), prefetch=(), grid=(1,),
         in_specs=None, out_specs=None, scratch=(), mebibytes=8):
    skip = len(prefetch) + len(inputs)

    def body(*refs):
        return kernel(*refs[:skip], *refs[skip + len(after) :])

    in_specs = in_specs or [WHOLE] * len(inputs)
    return pl.pallas_call(
        body,
        out_shape=out_shape,
        grid_spec=pltpu.PrefetchScalarGridSpec(
            num_scalar_prefetch=len(prefetch),
            grid=grid,
            in_specs=[*in_specs, *[pl.BlockSpec(memory_space=pl.ANY)] * len(after)],
            out_specs=out_specs or WHOLE,
            scratch_shapes=scratch,
        ),
        compiler_params=pltpu.CompilerParams(vmem_limit_bytes=mebibytes << 20),
        cost_estimate=pl.CostEstimate(
            flops=int(micros * 1.1e9), bytes_accessed=0, transcendentals=0
        ),
        name=name,
    )(*prefetch, *inputs, *after)


def stage(layer):
    return pl.when(layer >= 0)


def in_hbm(array):
    return pltpu.with_memory_space_constraint(array, pltpu.HBM)


def hold(array, after):
    return pl.pallas_call(
        lambda *refs: None,
        out_shape=jax.ShapeDtypeStruct(array.shape, array.dtype),
        in_specs=[WHOLE, *[pl.BlockSpec(memory_space=pl.ANY)] * len(after)],
        out_specs=WHOLE,
        input_output_aliases={0: 0},
        compiler_params=pltpu.CompilerParams(vmem_limit_bytes=1 << 20),
        cost_estimate=pl.CostEstimate(flops=0, bytes_accessed=0, transcendentals=0),
        name="hold",
    )(array, *after)


def side_kernel(layer_ref, grads_ref, proj_ref, out_ref):
    side = lax.dot_general(grads_ref[0, 0], proj_ref[0], NT, preferred_element_type=F32)
    out_ref[0] = side.T


def side_partial(layer, grads, out_proj, micros, after=()):
    _, count, length, feats = grads.shape
    rank = out_proj.shape[1]
    return call(
        side_kernel,
        [grads, out_proj],
        jax.ShapeDtypeStruct((count, rank, length), F32),
        "side_partial",
        micros=micros,
        after=after,
        prefetch=[layer],
        grid=(count,),
        in_specs=[
            pl.BlockSpec((1, 1, length, feats), lambda i, l: (l[0], i, 0, 0)),
            pl.BlockSpec((1, rank, feats), lambda i, l: (l[0], 0, 0)),
        ],
        out_specs=pl.BlockSpec((1, rank, length), lambda i, l: (i, 0, 0)),
    )


def sides_of(layer, grads_ref, proj_ref, out_ref):
    for seq in range(out_ref.shape[0]):
        out_ref[seq] = lax.dot_general(
            grads_ref[layer, seq], proj_ref[layer], NT, preferred_element_type=F32
        ).T


def sides_kernel(layer_ref, grads_ref, proj_ref, out_ref):
    sides_of(layer_ref[0], grads_ref, proj_ref, out_ref)


def sides_partial(layer, grads, out_proj, micros, after=()):
    _, count, length, feats = grads.shape
    return call(
        sides_kernel,
        [grads, out_proj],
        jax.ShapeDtypeStruct((count, out_proj.shape[1], length), F32),
        "sides_partial",
        micros=micros,
        after=after,
        prefetch=[layer],
        mebibytes=4,
    )


def both_kernel(
    layer_ref, ids_ref, acts_ref, in_proj_ref, table_ref, grads_ref, proj_ref,
    in_ref, scale_ref, out_ref,
):
    for at in range(acts_ref.shape[0]):
        for seq in range(acts_ref.shape[1]):
            in_side_of(acts_ref.at[at, seq], in_proj_ref.at[at], in_ref, (at, seq))
    token_kernel(ids_ref, table_ref, scale_ref)
    sides_of(layer_ref[0], grads_ref, proj_ref, out_ref)


def query_in_and_side(
    layer, ids, acts, in_proj, token_weight, grads, out_proj, micros, after=()
):
    layers, acts_n, length, feats = acts.shape
    _, heads, rank, width = in_proj.shape
    count = grads.shape[1]
    return call(
        both_kernel,
        [ids, acts, in_proj, token_table(token_weight), grads, out_proj],
        [
            jax.ShapeDtypeStruct((layers, acts_n, length, heads * rank), BF16),
            jax.ShapeDtypeStruct(ids.shape, F32),
            jax.ShapeDtypeStruct((count, rank, length), F32),
        ],
        "query_in_and_side",
        micros=micros,
        after=after,
        mebibytes=8,
        prefetch=[layer],
        out_specs=[WHOLE] * 3,
    )


def first_kernel(layer_ref, grads_hbm, proj_hbm, out_ref, grads, proj, sems):
    layer = layer_ref[0]
    copies = [
        pltpu.make_async_copy(proj_hbm.at[layer], proj, sems.at[0]),
        pltpu.make_async_copy(grads_hbm.at[layer], grads, sems.at[1]),
    ]
    for copy in copies:
        copy.start()
    for copy in copies:
        copy.wait()

    @stage(layer)
    def _():
        for seq in range(grads.shape[0]):
            out_ref[seq] = lax.dot_general(
                grads[seq], proj[...], NT, preferred_element_type=F32
            ).T


def first_partial(layer, grads, out_proj, micros):
    _, count, length, feats = grads.shape
    rank = out_proj.shape[1]
    return call(
        first_kernel,
        [in_hbm(grads), in_hbm(out_proj)],
        jax.ShapeDtypeStruct((count, rank, length), F32),
        "first_partial",
        micros=micros,
        prefetch=[layer],
        in_specs=[IN_HBM, IN_HBM],
        scratch=[
            pltpu.VMEM((count, length, feats), BF16),
            pltpu.VMEM((rank, feats), BF16),
            pltpu.SemaphoreType.DMA((2,)),
        ],
    )


def in_side_of(acts, proj, out_ref, at):
    heads, rank, width = proj.shape
    none = jnp.zeros((rank, width), BF16)
    for pair in range(heads // 2):
        one, two = proj[2 * pair], proj[2 * pair + 1]
        both = jnp.concatenate(
            [jnp.concatenate([one, none], axis=1), jnp.concatenate([none, two], axis=1)], axis=0
        )
        pair_acts = acts[:, 2 * width * pair : 2 * width * (pair + 1)]
        side = lax.dot_general(pair_acts, both, NT, preferred_element_type=F32)
        out_ref[(*at, slice(None), slice(2 * rank * pair, 2 * rank * (pair + 1)))] = side.astype(
            BF16
        )


def in_kernel(acts_ref, proj_ref, out_ref):
    in_side_of(acts_ref.at[0, 0], proj_ref.at[0], out_ref, (0, 0))


def in_side(acts, in_proj, micros, after=()):
    layers, count, length, feats = acts.shape
    _, heads, rank, width = in_proj.shape
    return call(
        in_kernel,
        [acts, in_proj],
        jax.ShapeDtypeStruct((layers, count, length, heads * rank), BF16),
        "in_side",
        micros=micros,
        after=after,
        grid=(layers, count),
        in_specs=[
            pl.BlockSpec((1, 1, length, feats), lambda l, i: (l, i, 0, 0)),
            pl.BlockSpec((1, heads, rank, width), lambda l, i: (l, 0, 0, 0)),
        ],
        out_specs=pl.BlockSpec((1, 1, length, heads * rank), lambda l, i: (l, i, 0, 0)),
    )


def layer_in_kernel(layer_ref, acts_ref, proj_ref, out_ref):
    layer = layer_ref[0]
    for seq in range(out_ref.shape[0]):
        in_side_of(acts_ref.at[layer, seq], proj_ref.at[layer], out_ref, (seq,))


def in_side_of_layer(layer, acts, in_proj, micros, after=()):
    _, count, length, _ = acts.shape
    _, heads, rank, _ = in_proj.shape
    return call(
        layer_in_kernel,
        [acts, in_proj],
        jax.ShapeDtypeStruct((count, length, heads * rank), BF16),
        "in_side_of_layer",
        micros=micros,
        prefetch=[layer],
        after=after,
    )


def stage_kernel(acts_hbm, out_ref, tick_ref, sems):
    layers, count = out_ref.shape[:2]
    copies = [
        pltpu.make_async_copy(
            acts_hbm.at[layer, seq], out_ref.at[layer, seq], sems.at[layer * count + seq]
        )
        for layer in range(layers)
        for seq in range(count)
    ]
    for copy in copies:
        copy.start()
    tick_ref[...] = jnp.zeros_like(tick_ref)
    for copy in copies:
        copy.wait()


def staged(acts, after):
    return call(
        stage_kernel,
        [in_hbm(acts)],
        [jax.ShapeDtypeStruct(acts.shape, BF16), jax.ShapeDtypeStruct((8, 128), F32)],
        "staged",
        micros=0.1,
        after=after,
        in_specs=[IN_HBM],
        out_specs=[WHOLE] * 2,
        scratch=[pltpu.SemaphoreType.DMA((acts.shape[0] * acts.shape[1],))],
    )


def settle_kernel(one_ref, two_ref, out_ref):
    out_ref[...] = one_ref[...] + two_ref[...]


def settle(one, two, after):
    return call(
        settle_kernel, [one, two], jax.ShapeDtypeStruct(one.shape, F32), "settle", micros=0.1,
        after=after,
    )


def token_kernel(ids_ref, table_ref, out_ref):
    table = table_ref[...]
    rows, lanes = table.shape
    high = table.astype(BF16)
    rest = table - high.astype(F32)
    mid = rest.astype(BF16)
    low = (rest - mid.astype(F32)).astype(BF16)
    turned = [part.T for part in (high, mid, low)]
    length = ids_ref.shape[1]
    for row in range(ids_ref.shape[0]):
        ids = ids_ref[row : row + 1, :]
        block = ids // lanes
        at = lax.broadcasted_iota(jnp.int32, (rows, length), 0) == block
        hot = jnp.where(at, 1.0, 0.0).astype(BF16)
        picked = sum(jnp.dot(part, hot, preferred_element_type=F32) for part in turned)
        lane = lax.broadcasted_iota(jnp.int32, (lanes, length), 0) == ids - block * lanes
        out_ref[row : row + 1, :] = jnp.sum(
            jnp.where(lane, picked, 0.0), axis=0, keepdims=True
        )


def token_table(token_weight):
    lanes = 128
    return jnp.pad(token_weight, (0, -token_weight.shape[0] % lanes)).reshape(-1, lanes)


def token_scale(ids, token_weight, micros, after=()):
    table = token_table(token_weight)
    return call(
        token_kernel,
        [ids, table],
        jax.ShapeDtypeStruct(ids.shape, F32),
        "token_scale",
        micros=micros,
        after=after,
    )


def blocks_of(side, scale, in_side_seq):
    weighted = (side * scale).astype(BF16)
    product = jnp.dot(weighted, in_side_seq, preferred_element_type=F32)
    return product * (1.0 / math.sqrt(side.shape[1]))


def ready_kernel(layer_ref, own_ref, other_ref, scale_ref, in_ref, *refs):
    out_factor_ref, in_factor_ref, *out_refs = refs
    layers, heads, rank, _ = in_factor_ref.shape
    none = jnp.zeros((rank, rank), F32)
    for layer in range(layers):
        lefts = []
        for seq in range(out_refs[layer].shape[0]):
            side = jnp.where(layer_ref[0] == layer, own_ref[seq], other_ref[seq])
            blocks = blocks_of(side, scale_ref[seq : seq + 1, :], in_ref[layer, seq])
            lefts.append(
                jnp.dot(out_factor_ref[layer], blocks, precision=HIGH, preferred_element_type=F32)
            )
        for pair in range(heads // 2):
            one, two = in_factor_ref[layer, 2 * pair], in_factor_ref[layer, 2 * pair + 1]
            both = jnp.concatenate(
                [jnp.concatenate([one, none], axis=1), jnp.concatenate([none, two], axis=1)],
                axis=0,
            )
            span = slice(2 * rank * pair, 2 * rank * (pair + 1))
            for seq, left in enumerate(lefts):
                out_refs[layer][seq, :, span] = jnp.dot(
                    left[:, span], both, precision=HIGH, preferred_element_type=F32
                )


def query_ready(layer, own, other, scale, in_sides, out_factor, in_factor, after=()):
    layers, count, _, wide = in_sides.shape
    rank = own.shape[1]
    return call(
        ready_kernel,
        [own, other, scale, in_sides, out_factor, in_factor],
        [jax.ShapeDtypeStruct((count, rank, wide), F32)] * layers,
        "query_ready",
        micros=0.1,
        prefetch=[layer],
        after=after,
        out_specs=[WHOLE] * layers,
    )


def score_kernel(layers, queries_n, sides_n, first, norm, at_ref, *refs):
    query_refs, refs = refs[:queries_n], refs[queries_n:]
    side_refs, refs = refs[:sides_n], refs[sides_n:]
    scale_ref, in_ref, *before_refs, out_ref = refs
    rows, lanes = out_ref.shape
    row_at = lax.broadcasted_iota(jnp.int32, (rows, lanes), 0)
    lane_at = lax.broadcasted_iota(jnp.int32, (rows, lanes), 1)
    total = jnp.zeros((rows, lanes), F32)
    for ref in before_refs:
        total = total + ref[...]
    queries = [(refs, idx) for refs in zip(*[iter(query_refs)] * layers) for idx in range(refs[0].shape[0])]
    sides = [(ref, idx) for ref in side_refs for idx in range(ref.shape[0])]
    for seq, (side_ref, side_idx) in enumerate(sides, first):
        blocks = blocks_of(side_ref[side_idx], scale_ref[seq : seq + 1, :], in_ref[seq])
        for row, (layer_refs, idx) in enumerate(queries):
            query = layer_refs[0][idx]
            for layer in range(1, layers):
                query = jnp.where(at_ref[0] == layer, layer_refs[layer][idx], query)
            product = jnp.sum(query * blocks, axis=0, keepdims=True)
            value = jnp.sum(product, axis=1, keepdims=True) * norm
            here = (row_at == (row ^ at_ref[1])) & (lane_at == seq)
            total = total + jnp.where(here, value, 0.0)
    out_ref[...] = total


def score_terms(layer, flip, norm, queries, sides, scale, in_sides, before=(), first=0, micros=1.5):
    layers = len(queries[0])
    rows = sum(query[0].shape[0] for query in queries)
    flat = [array for query in queries for array in query]
    return call(
        functools.partial(score_kernel, layers, len(flat), len(sides), first, norm),
        [*flat, *sides, scale, in_sides, *before],
        jax.ShapeDtypeStruct((rows, 128), F32),
        "score_terms",
        micros=micros,
        prefetch=[jnp.concatenate([layer, flip])],
    )


def lever_kernel(layers, queries_n, layer_ref, *refs):
    query_refs, (in_ref, out_ref) = refs[:queries_n], refs[queries_n:]
    rows = []
    for layer_refs in zip(*[iter(query_refs)] * layers):
        for idx in range(layer_refs[0].shape[0]):
            query = layer_refs[0][idx]
            for layer in range(1, layers):
                query = jnp.where(layer_ref[0] == layer, layer_refs[layer][idx], query)
            rows.append(query.astype(BF16))
    stacked = jnp.concatenate(rows, axis=0)
    for seq in range(in_ref.shape[0]):
        out_ref[seq] = lax.dot_general(stacked, in_ref[seq], NT, preferred_element_type=F32)


def query_levers(layer, queries, in_sides):
    flat = [array for query in queries for array in query]
    rows = sum(query[0].shape[0] * query[0].shape[1] for query in queries)
    count, length, _ = in_sides.shape
    return call(
        functools.partial(lever_kernel, len(queries[0]), len(flat)),
        [*flat, in_sides],
        jax.ShapeDtypeStruct((count, rows, length), F32),
        "query_levers",
        micros=1.5,
        prefetch=[layer],
    )


def lever_score_kernel(norm, flip_ref, lever_ref, side_ref, scale_ref, before_ref, out_ref):
    rows, lanes = out_ref.shape
    rank = side_ref.shape[1]
    row_at = lax.broadcasted_iota(jnp.int32, (rows, lanes), 0)
    lane_at = lax.broadcasted_iota(jnp.int32, (rows, lanes), 1)
    total = before_ref[...]
    for seq in range(side_ref.shape[0]):
        weighted = (side_ref[seq] * scale_ref[seq : seq + 1, :]).astype(BF16).astype(F32)
        for row in range(rows):
            product = lever_ref[seq, rank * row : rank * (row + 1), :] * weighted
            value = jnp.sum(jnp.sum(product, axis=0, keepdims=True), axis=1, keepdims=True)
            here = (row_at == (row ^ flip_ref[0])) & (lane_at == seq)
            total = total + jnp.where(here, value * norm, 0.0)
    out_ref[...] = total


def lever_scores(flip, norm, levers, side, scale, before):
    return call(
        functools.partial(lever_score_kernel, norm / math.sqrt(side.shape[2])),
        [levers, side, scale, before],
        jax.ShapeDtypeStruct(before.shape, F32),
        "lever_scores",
        micros=0.5,
        prefetch=[flip],
    )


def local(
    train_grads,
    train_acts,
    train_ids,
    query_grads,
    query_acts,
    query_ids,
    token_weight,
    out_proj,
    in_proj,
    out_factor,
    in_factor,
):
    layers, train_n = train_grads.shape[:2]
    query_n = query_ids.shape[0]
    heads, rank = in_proj.shape[1:3]
    n_head, n_dp = lax.axis_size("head"), lax.axis_size("dp")
    by_pairs = n_head == 4 and n_dp == 4 and layers == 2 and query_n == 1
    norm = 1.0 / math.sqrt(layers * heads * n_head * rank * rank)

    def scalar(idx):
        return jnp.asarray(idx, jnp.int32).reshape(1)

    def near(array, axis="head"):
        return lax.ppermute(array, axis, NEAR)

    def far(array, axis="head"):
        return lax.ppermute(array, axis, FAR)

    if by_pairs:
        mine = scalar(lax.axis_index("head") % 2)
        other = 1 - mine
        flip = scalar(lax.axis_index("dp"))
        query_out = first_partial(other, query_grads, out_proj, 8.0)
        query_got = near(query_out)
        train_out = sides_partial(other, train_grads, out_proj, 2.0, [query_out])
        query_keep = sides_partial(mine, query_grads, out_proj, 0.5, [train_out])
        query_pair = query_keep + query_got
        query_far = far(query_pair)
        train_got = near(hold(train_out, [query_pair]))
        query_in, query_scale, train_keep = query_in_and_side(
            mine, query_ids, query_acts, in_proj, token_weight, train_grads, out_proj, 3.0,
            [query_pair],
        )
        query_own = settle(query_pair, query_far, [query_scale])
        query_other = near(query_own)
        parts = [(i * train_n // 1, (i + 1) * train_n // 1) for i in range(1)]
        pairs = [train_keep[a:b] + train_got[a:b] for a, b in parts]
        ready = query_ready(
            mine, query_own, query_other, query_scale, query_in, out_factor, in_factor, pairs
        )
        across = [far(one, "dp") for one in ready]
        train_scale = token_scale(train_ids, token_weight, 0.1, ready[-1:])
        acts, tick = staged(train_acts, [train_scale])
        owns = [pair + hold(far(pair), [tick]) for pair in pairs]
        others = [near(own) for own in owns]
        in_other = in_side_of_layer(other, acts, in_proj, 2.5, owns)
        across = [hold(across[0], [owns[0]]), hold(across[1], [owns[0]])]
        in_own = in_side_of_layer(mine, acts, in_proj, 6.0, [in_other])
        every = [
            ready,
            [near(one, "dp") for one in ready],
            across,
            [near(one, "dp") for one in across],
        ]
        terms = score_terms(mine, flip, norm, every, owns, train_scale, in_own)
        levers = query_levers(other, every, in_other)
        terms = lever_scores(flip, norm, levers, others[0], train_scale, terms)
        total = terms
        for shift in range(1, 4):
            total = total + lax.ppermute(
                terms, "head", [(idx, (idx + shift) % 4) for idx in range(4)]
            )
    else:
        query_scale = token_scale(query_ids, token_weight, 0.5)
        train_scale = token_scale(train_ids, token_weight, 1.5)
        query_in = in_side(query_acts, in_proj, 0.9)
        train_in = in_side(train_acts, in_proj, 3.5)
        at = [scalar(idx) for idx in range(layers)]
        query_sides, train_sides = lax.psum(
            (
                [side_partial(idx, query_grads, out_proj, 0.5) for idx in at],
                [side_partial(idx, train_grads, out_proj, 1.9) for idx in at],
            ),
            "head",
        )
        ready = query_ready(
            at[0], *query_sides, query_scale, query_in, out_factor, in_factor
        )
        every = [[lax.all_gather(one, "dp", axis=0, tiled=True) for one in ready]]
        terms = []
        for layer, idx in enumerate(at):
            sides, in_sides = train_sides[layer], train_in[layer]
            before = terms[-1:]
            terms.append(
                score_terms(idx, scalar(0), norm, every, [sides], train_scale, in_sides, before)
            )
        total = lax.psum(terms[-1], "head")
    return total[:, :train_n]


def solution(mesh):
    return jax.shard_map(
        local,
        mesh=mesh,
        in_specs=(
            P(None, ("groups", "dp"), None, "head"),
            P(None, ("groups", "dp"), None, "head"),
            P(("groups", "dp"), None),
            P(None, ("groups", "dp"), None, "head"),
            P(None, ("groups", "dp"), None, "head"),
            P(("groups", "dp"), None),
            P(),
            P(None, None, "head"),
            P(None, "head", None, None),
            P(),
            P(None, "head", None, None),
        ),
        out_specs=P(None, ("groups", "dp")),
        check_vma=False,
    )
```

```python
import functools
import math

import jax
import jax.numpy as jnp
from jax import lax
from jax.experimental import pallas as pl
from jax.experimental.pallas import tpu as pltpu
from jax.sharding import PartitionSpec as P

HIGH = lax.Precision.HIGHEST
F32 = jnp.float32
BF16 = jnp.bfloat16
NT = (((1,), (1,)), ((), ()))

NEAR = [(0, 1), (1, 0), (2, 3), (3, 2)]
FAR = [(0, 2), (2, 0), (1, 3), (3, 1)]

WHOLE = pl.BlockSpec(memory_space=pltpu.VMEM)
IN_HBM = pl.BlockSpec(memory_space=pltpu.HBM)


def call(kernel, inputs, out_shape, name, *, micros, after=(), prefetch=(), grid=(1,),
         in_specs=None, out_specs=None, scratch=(), mebibytes=8):
    skip = len(prefetch) + len(inputs)

    def body(*refs):
        return kernel(*refs[:skip], *refs[skip + len(after) :])

    in_specs = in_specs or [WHOLE] * len(inputs)
    return pl.pallas_call(
        body,
        out_shape=out_shape,
        grid_spec=pltpu.PrefetchScalarGridSpec(
            num_scalar_prefetch=len(prefetch),
            grid=grid,
            in_specs=[*in_specs, *[pl.BlockSpec(memory_space=pl.ANY)] * len(after)],
            out_specs=out_specs or WHOLE,
            scratch_shapes=scratch,
        ),
        compiler_params=pltpu.CompilerParams(vmem_limit_bytes=mebibytes << 20),
        cost_estimate=pl.CostEstimate(
            flops=int(micros * 1.1e9), bytes_accessed=0, transcendentals=0
        ),
        name=name,
    )(*prefetch, *inputs, *after)


def stage(layer):
    return pl.when(layer >= 0)


def in_hbm(array):
    return pltpu.with_memory_space_constraint(array, pltpu.HBM)


def hold(array, after):
    return pl.pallas_call(
        lambda *refs: None,
        out_shape=jax.ShapeDtypeStruct(array.shape, array.dtype),
        in_specs=[WHOLE, *[pl.BlockSpec(memory_space=pl.ANY)] * len(after)],
        out_specs=WHOLE,
        input_output_aliases={0: 0},
        compiler_params=pltpu.CompilerParams(vmem_limit_bytes=1 << 20),
        cost_estimate=pl.CostEstimate(flops=0, bytes_accessed=0, transcendentals=0),
        name="hold",
    )(array, *after)


def side_kernel(layer_ref, grads_ref, proj_ref, out_ref):
    side = lax.dot_general(grads_ref[0, 0], proj_ref[0], NT, preferred_element_type=F32)
    out_ref[0] = side.T


def side_partial(layer, grads, out_proj, micros, after=()):
    _, count, length, feats = grads.shape
    rank = out_proj.shape[1]
    return call(
        side_kernel,
        [grads, out_proj],
        jax.ShapeDtypeStruct((count, rank, length), F32),
        "side_partial",
        micros=micros,
        after=after,
        prefetch=[layer],
        grid=(count,),
        in_specs=[
            pl.BlockSpec((1, 1, length, feats), lambda i, l: (l[0], i, 0, 0)),
            pl.BlockSpec((1, rank, feats), lambda i, l: (l[0], 0, 0)),
        ],
        out_specs=pl.BlockSpec((1, rank, length), lambda i, l: (i, 0, 0)),
    )


def sides_of(layer, grads_ref, proj_ref, out_ref):
    for seq in range(out_ref.shape[0]):
        out_ref[seq] = lax.dot_general(
            grads_ref[layer, seq], proj_ref[layer], NT, preferred_element_type=F32
        ).T


def sides_kernel(layer_ref, grads_ref, proj_ref, out_ref):
    sides_of(layer_ref[0], grads_ref, proj_ref, out_ref)


def sides_partial(layer, grads, out_proj, micros, after=()):
    _, count, length, feats = grads.shape
    return call(
        sides_kernel,
        [grads, out_proj],
        jax.ShapeDtypeStruct((count, out_proj.shape[1], length), F32),
        "sides_partial",
        micros=micros,
        after=after,
        prefetch=[layer],
        mebibytes=4,
    )


def both_kernel(
    layer_ref, ids_ref, acts_ref, in_proj_ref, table_ref, grads_ref, proj_ref,
    in_ref, scale_ref, out_ref,
):
    for at in range(acts_ref.shape[0]):
        for seq in range(acts_ref.shape[1]):
            in_side_of(acts_ref.at[at, seq], in_proj_ref.at[at], in_ref, (at, seq))
    token_kernel(ids_ref, table_ref, scale_ref)
    sides_of(layer_ref[0], grads_ref, proj_ref, out_ref)


def query_in_and_side(
    layer, ids, acts, in_proj, token_weight, grads, out_proj, micros, after=()
):
    layers, acts_n, length, feats = acts.shape
    _, heads, rank, width = in_proj.shape
    count = grads.shape[1]
    return call(
        both_kernel,
        [ids, acts, in_proj, token_table(token_weight), grads, out_proj],
        [
            jax.ShapeDtypeStruct((layers, acts_n, length, heads * rank), BF16),
            jax.ShapeDtypeStruct(ids.shape, F32),
            jax.ShapeDtypeStruct((count, rank, length), F32),
        ],
        "query_in_and_side",
        micros=micros,
        after=after,
        mebibytes=8,
        prefetch=[layer],
        out_specs=[WHOLE] * 3,
    )


def first_kernel(layer_ref, grads_hbm, proj_hbm, out_ref, grads, proj, sems):
    layer = layer_ref[0]
    copies = [
        pltpu.make_async_copy(proj_hbm.at[layer], proj, sems.at[0]),
        pltpu.make_async_copy(grads_hbm.at[layer], grads, sems.at[1]),
    ]
    for copy in copies:
        copy.start()
    for copy in copies:
        copy.wait()

    @stage(layer)
    def _():
        for seq in range(grads.shape[0]):
            out_ref[seq] = lax.dot_general(
                grads[seq], proj[...], NT, preferred_element_type=F32
            ).T


def first_partial(layer, grads, out_proj, micros):
    _, count, length, feats = grads.shape
    rank = out_proj.shape[1]
    return call(
        first_kernel,
        [in_hbm(grads), in_hbm(out_proj)],
        jax.ShapeDtypeStruct((count, rank, length), F32),
        "first_partial",
        micros=micros,
        prefetch=[layer],
        in_specs=[IN_HBM, IN_HBM],
        scratch=[
            pltpu.VMEM((count, length, feats), BF16),
            pltpu.VMEM((rank, feats), BF16),
            pltpu.SemaphoreType.DMA((2,)),
        ],
    )


def in_side_of(acts, proj, out_ref, at):
    heads, rank, width = proj.shape
    none = jnp.zeros((rank, width), BF16)
    for pair in range(heads // 2):
        one, two = proj[2 * pair], proj[2 * pair + 1]
        both = jnp.concatenate(
            [jnp.concatenate([one, none], axis=1), jnp.concatenate([none, two], axis=1)], axis=0
        )
        pair_acts = acts[:, 2 * width * pair : 2 * width * (pair + 1)]
        side = lax.dot_general(pair_acts, both, NT, preferred_element_type=F32)
        out_ref[(*at, slice(None), slice(2 * rank * pair, 2 * rank * (pair + 1)))] = side.astype(
            BF16
        )


def in_kernel(acts_ref, proj_ref, out_ref):
    in_side_of(acts_ref.at[0, 0], proj_ref.at[0], out_ref, (0, 0))


def in_side(acts, in_proj, micros, after=()):
    layers, count, length, feats = acts.shape
    _, heads, rank, width = in_proj.shape
    return call(
        in_kernel,
        [acts, in_proj],
        jax.ShapeDtypeStruct((layers, count, length, heads * rank), BF16),
        "in_side",
        micros=micros,
        after=after,
        grid=(layers, count),
        in_specs=[
            pl.BlockSpec((1, 1, length, feats), lambda l, i: (l, i, 0, 0)),
            pl.BlockSpec((1, heads, rank, width), lambda l, i: (l, 0, 0, 0)),
        ],
        out_specs=pl.BlockSpec((1, 1, length, heads * rank), lambda l, i: (l, i, 0, 0)),
    )


def layer_in_kernel(layer_ref, acts_ref, proj_ref, out_ref):
    layer = layer_ref[0]
    for seq in range(out_ref.shape[0]):
        in_side_of(acts_ref.at[layer, seq], proj_ref.at[layer], out_ref, (seq,))


def in_side_of_layer(layer, acts, in_proj, micros, after=()):
    _, count, length, _ = acts.shape
    _, heads, rank, _ = in_proj.shape
    return call(
        layer_in_kernel,
        [acts, in_proj],
        jax.ShapeDtypeStruct((count, length, heads * rank), BF16),
        "in_side_of_layer",
        micros=micros,
        prefetch=[layer],
        after=after,
    )


def stage_kernel(acts_hbm, out_ref, tick_ref, sems):
    layers, count = out_ref.shape[:2]
    copies = [
        pltpu.make_async_copy(
            acts_hbm.at[layer, seq], out_ref.at[layer, seq], sems.at[layer * count + seq]
        )
        for layer in range(layers)
        for seq in range(count)
    ]
    for copy in copies:
        copy.start()
    tick_ref[...] = jnp.zeros_like(tick_ref)
    for copy in copies:
        copy.wait()


def staged(acts, after):
    return call(
        stage_kernel,
        [in_hbm(acts)],
        [jax.ShapeDtypeStruct(acts.shape, BF16), jax.ShapeDtypeStruct((8, 128), F32)],
        "staged",
        micros=0.1,
        after=after,
        in_specs=[IN_HBM],
        out_specs=[WHOLE] * 2,
        scratch=[pltpu.SemaphoreType.DMA((acts.shape[0] * acts.shape[1],))],
    )


def settle_kernel(one_ref, two_ref, out_ref):
    out_ref[...] = one_ref[...] + two_ref[...]


def settle(one, two, after):
    return call(
        settle_kernel, [one, two], jax.ShapeDtypeStruct(one.shape, F32), "settle", micros=0.1,
        after=after,
    )


def token_kernel(ids_ref, table_ref, out_ref):
    table = table_ref[...]
    rows, lanes = table.shape
    high = table.astype(BF16)
    rest = table - high.astype(F32)
    mid = rest.astype(BF16)
    low = (rest - mid.astype(F32)).astype(BF16)
    turned = [part.T for part in (high, mid, low)]
    length = ids_ref.shape[1]
    for row in range(ids_ref.shape[0]):
        ids = ids_ref[row : row + 1, :]
        block = ids // lanes
        at = lax.broadcasted_iota(jnp.int32, (rows, length), 0) == block
        hot = jnp.where(at, 1.0, 0.0).astype(BF16)
        picked = sum(jnp.dot(part, hot, preferred_element_type=F32) for part in turned)
        lane = lax.broadcasted_iota(jnp.int32, (lanes, length), 0) == ids - block * lanes
        out_ref[row : row + 1, :] = jnp.sum(
            jnp.where(lane, picked, 0.0), axis=0, keepdims=True
        )


def token_table(token_weight):
    lanes = 128
    return jnp.pad(token_weight, (0, -token_weight.shape[0] % lanes)).reshape(-1, lanes)


def token_scale(ids, token_weight, micros, after=()):
    table = token_table(token_weight)
    return call(
        token_kernel,
        [ids, table],
        jax.ShapeDtypeStruct(ids.shape, F32),
        "token_scale",
        micros=micros,
        after=after,
    )


def blocks_of(side, scale, in_side_seq):
    weighted = (side * scale).astype(BF16)
    product = jnp.dot(weighted, in_side_seq, preferred_element_type=F32)
    return product * (1.0 / math.sqrt(side.shape[1]))


def ready_kernel(layer_ref, own_ref, other_ref, scale_ref, in_ref, *refs):
    out_factor_ref, in_factor_ref, *out_refs = refs
    layers, heads, rank, _ = in_factor_ref.shape
    none = jnp.zeros((rank, rank), F32)
    for layer in range(layers):
        lefts = []
        for seq in range(out_refs[layer].shape[0]):
            side = jnp.where(layer_ref[0] == layer, own_ref[seq], other_ref[seq])
            blocks = blocks_of(side, scale_ref[seq : seq + 1, :], in_ref[layer, seq])
            lefts.append(
                jnp.dot(out_factor_ref[layer], blocks, precision=HIGH, preferred_element_type=F32)
            )
        for pair in range(heads // 2):
            one, two = in_factor_ref[layer, 2 * pair], in_factor_ref[layer, 2 * pair + 1]
            both = jnp.concatenate(
                [jnp.concatenate([one, none], axis=1), jnp.concatenate([none, two], axis=1)],
                axis=0,
            )
            span = slice(2 * rank * pair, 2 * rank * (pair + 1))
            for seq, left in enumerate(lefts):
                out_refs[layer][seq, :, span] = jnp.dot(
                    left[:, span], both, precision=HIGH, preferred_element_type=F32
                )


def query_ready(layer, own, other, scale, in_sides, out_factor, in_factor, after=()):
    layers, count, _, wide = in_sides.shape
    rank = own.shape[1]
    return call(
        ready_kernel,
        [own, other, scale, in_sides, out_factor, in_factor],
        [jax.ShapeDtypeStruct((count, rank, wide), F32)] * layers,
        "query_ready",
        micros=0.1,
        prefetch=[layer],
        after=after,
        out_specs=[WHOLE] * layers,
    )


def score_kernel(layers, queries_n, sides_n, first, norm, at_ref, *refs):
    query_refs, refs = refs[:queries_n], refs[queries_n:]
    side_refs, refs = refs[:sides_n], refs[sides_n:]
    scale_ref, in_ref, *before_refs, out_ref = refs
    rows, lanes = out_ref.shape
    row_at = lax.broadcasted_iota(jnp.int32, (rows, lanes), 0)
    lane_at = lax.broadcasted_iota(jnp.int32, (rows, lanes), 1)
    total = jnp.zeros((rows, lanes), F32)
    for ref in before_refs:
        total = total + ref[...]
    queries = [(refs, idx) for refs in zip(*[iter(query_refs)] * layers) for idx in range(refs[0].shape[0])]
    sides = [(ref, idx) for ref in side_refs for idx in range(ref.shape[0])]
    for seq, (side_ref, side_idx) in enumerate(sides, first):
        blocks = blocks_of(side_ref[side_idx], scale_ref[seq : seq + 1, :], in_ref[seq])
        for row, (layer_refs, idx) in enumerate(queries):
            query = layer_refs[0][idx]
            for layer in range(1, layers):
                query = jnp.where(at_ref[0] == layer, layer_refs[layer][idx], query)
            product = jnp.sum(query * blocks, axis=0, keepdims=True)
            value = jnp.sum(product, axis=1, keepdims=True) * norm
            here = (row_at == (row ^ at_ref[1])) & (lane_at == seq)
            total = total + jnp.where(here, value, 0.0)
    out_ref[...] = total


def score_terms(layer, flip, norm, queries, sides, scale, in_sides, before=(), first=0, micros=1.5):
    layers = len(queries[0])
    rows = sum(query[0].shape[0] for query in queries)
    flat = [array for query in queries for array in query]
    return call(
        functools.partial(score_kernel, layers, len(flat), len(sides), first, norm),
        [*flat, *sides, scale, in_sides, *before],
        jax.ShapeDtypeStruct((rows, 128), F32),
        "score_terms",
        micros=micros,
        prefetch=[jnp.concatenate([layer, flip])],
    )


def lever_kernel(layers, queries_n, layer_ref, *refs):
    query_refs, (in_ref, out_ref) = refs[:queries_n], refs[queries_n:]
    rows = []
    for layer_refs in zip(*[iter(query_refs)] * layers):
        for idx in range(layer_refs[0].shape[0]):
            query = layer_refs[0][idx]
            for layer in range(1, layers):
                query = jnp.where(layer_ref[0] == layer, layer_refs[layer][idx], query)
            rows.append(query.astype(BF16))
    stacked = jnp.concatenate(rows, axis=0)
    for seq in range(in_ref.shape[0]):
        out_ref[seq] = lax.dot_general(stacked, in_ref[seq], NT, preferred_element_type=F32)


def query_levers(layer, queries, in_sides):
    flat = [array for query in queries for array in query]
    rows = sum(query[0].shape[0] * query[0].shape[1] for query in queries)
    count, length, _ = in_sides.shape
    return call(
        functools.partial(lever_kernel, len(queries[0]), len(flat)),
        [*flat, in_sides],
        jax.ShapeDtypeStruct((count, rows, length), F32),
        "query_levers",
        micros=1.5,
        prefetch=[layer],
    )


def lever_score_kernel(norm, flip_ref, lever_ref, side_ref, scale_ref, before_ref, out_ref):
    rows, lanes = out_ref.shape
    rank = side_ref.shape[1]
    row_at = lax.broadcasted_iota(jnp.int32, (rows, lanes), 0)
    lane_at = lax.broadcasted_iota(jnp.int32, (rows, lanes), 1)
    total = before_ref[...]
    for seq in range(side_ref.shape[0]):
        weighted = (side_ref[seq] * scale_ref[seq : seq + 1, :]).astype(BF16).astype(F32)
        for row in range(rows):
            product = lever_ref[seq, rank * row : rank * (row + 1), :] * weighted
            value = jnp.sum(jnp.sum(product, axis=0, keepdims=True), axis=1, keepdims=True)
            here = (row_at == (row ^ flip_ref[0])) & (lane_at == seq)
            total = total + jnp.where(here, value * norm, 0.0)
    out_ref[...] = total


def lever_scores(flip, norm, levers, side, scale, before):
    return call(
        functools.partial(lever_score_kernel, norm / math.sqrt(side.shape[2])),
        [levers, side, scale, before],
        jax.ShapeDtypeStruct(before.shape, F32),
        "lever_scores",
        micros=0.5,
        prefetch=[flip],
    )


def local(
    train_grads,
    train_acts,
    train_ids,
    query_grads,
    query_acts,
    query_ids,
    token_weight,
    out_proj,
    in_proj,
    out_factor,
    in_factor,
):
    layers, train_n = train_grads.shape[:2]
    query_n = query_ids.shape[0]
    heads, rank = in_proj.shape[1:3]
    n_head, n_dp = lax.axis_size("head"), lax.axis_size("dp")
    by_pairs = n_head == 4 and n_dp == 4 and layers == 2 and query_n == 1
    norm = 1.0 / math.sqrt(layers * heads * n_head * rank * rank)

    def scalar(idx):
        return jnp.asarray(idx, jnp.int32).reshape(1)

    def near(array, axis="head"):
        return lax.ppermute(array, axis, NEAR)

    def far(array, axis="head"):
        return lax.ppermute(array, axis, FAR)

    if by_pairs:
        mine = scalar(lax.axis_index("head") % 2)
        other = 1 - mine
        flip = scalar(lax.axis_index("dp"))
        query_out = first_partial(other, query_grads, out_proj, 8.0)
        query_got = near(query_out)
        train_out = sides_partial(other, train_grads, out_proj, 2.0, [query_out])
        query_keep = sides_partial(mine, query_grads, out_proj, 0.5, [train_out])
        query_pair = query_keep + query_got
        query_far = far(query_pair)
        train_got = near(hold(train_out, [query_pair]))
        query_in, query_scale, train_keep = query_in_and_side(
            mine, query_ids, query_acts, in_proj, token_weight, train_grads, out_proj, 3.0,
            [query_pair],
        )
        query_own = settle(query_pair, query_far, [query_scale])
        query_other = near(query_own)
        parts = [(i * train_n // 1, (i + 1) * train_n // 1) for i in range(1)]
        pairs = [train_keep[a:b] + train_got[a:b] for a, b in parts]
        ready = query_ready(
            mine, query_own, query_other, query_scale, query_in, out_factor, in_factor, pairs
        )
        across = [far(one, "dp") for one in ready]
        train_scale = token_scale(train_ids, token_weight, 0.1, ready[-1:])
        acts, tick = staged(train_acts, [train_scale])
        owns = [pair + hold(far(pair), [tick]) for pair in pairs]
        others = [near(own) for own in owns]
        in_other = in_side_of_layer(other, acts, in_proj, 2.5, owns)
        across = [hold(across[0], [owns[0]]), hold(across[1], [owns[0]])]
        in_own = in_side_of_layer(mine, acts, in_proj, 6.0, [in_other])
        every = [
            ready,
            [near(one, "dp") for one in ready],
            across,
            [near(one, "dp") for one in across],
        ]
        terms = lever_scores(
            flip, norm, query_levers(mine, every, in_own), owns[0], train_scale,
            jnp.zeros((n_dp, 128), F32),
        )
        levers = query_levers(other, every, in_other)
        terms = lever_scores(flip, norm, levers, others[0], train_scale, terms)
        total = terms
        for shift in range(1, 4):
            total = total + lax.ppermute(
                terms, "head", [(idx, (idx + shift) % 4) for idx in range(4)]
            )
    else:
        query_scale = token_scale(query_ids, token_weight, 0.5)
        train_scale = token_scale(train_ids, token_weight, 1.5)
        query_in = in_side(query_acts, in_proj, 0.9)
        train_in = in_side(train_acts, in_proj, 3.5)
        at = [scalar(idx) for idx in range(layers)]
        query_sides, train_sides = lax.psum(
            (
                [side_partial(idx, query_grads, out_proj, 0.5) for idx in at],
                [side_partial(idx, train_grads, out_proj, 1.9) for idx in at],
            ),
            "head",
        )
        ready = query_ready(
            at[0], *query_sides, query_scale, query_in, out_factor, in_factor
        )
        every = [[lax.all_gather(one, "dp", axis=0, tiled=True) for one in ready]]
        terms = []
        for layer, idx in enumerate(at):
            sides, in_sides = train_sides[layer], train_in[layer]
            before = terms[-1:]
            terms.append(
                score_terms(idx, scalar(0), norm, every, [sides], train_scale, in_sides, before)
            )
        total = lax.psum(terms[-1], "head")
    return total[:, :train_n]


def solution(mesh):
    return jax.shard_map(
        local,
        mesh=mesh,
        in_specs=(
            P(None, ("groups", "dp"), None, "head"),
            P(None, ("groups", "dp"), None, "head"),
            P(("groups", "dp"), None),
            P(None, ("groups", "dp"), None, "head"),
            P(None, ("groups", "dp"), None, "head"),
            P(("groups", "dp"), None),
            P(),
            P(None, None, "head"),
            P(None, "head", None, None),
            P(),
            P(None, "head", None, None),
        ),
        out_specs=P(None, ("groups", "dp")),
        check_vma=False,
    )
```
